32 devices in a mesh: space: 16 (over z, y, core), band: 2 (over x).
Axes of the slice: x: 2, y: 2, z: 4, core: 2. Of those that a mesh axis runs over, the one named last changes fastest.
Arguments:
- bands: bfloat16 [4, 4, 32, 128, 128], P('band', None, 'space'), may hold values from -6 to 6
- occ_level: int32 [4], P('band'), may hold values from 1 to 4
- block_owner: int32 [1], replicated, may hold values from 0 to 3
Outputs:
- exchange: float32 [2, 4, 32, 128, 128], P(None, None, 'space', 'band')
The draws below stay inside these ranges and needn't reach their ends.
All inputs are finite; a program needn't handle non-finite values.
Results may differ from the reference program's by a relative error of at most 0.0013.
Values may be sent and summed in bfloat16 or wider, within the bound.
A program may use at most 64 MiB of HBM per device.

```python
import jax
import jax.numpy as jnp
from jax import lax

NX = 128
NY = 128
RES_DEV = 2
BLOCK = 2
SWEEPS = 4
NZ = 32
BANDS = 4


def place_ends(array, rng, low, largest):
    longest = array.shape.index(max(array.shape))
    spots = []
    for shift in (0, 1):
        where = [jax.random.randint(jax.random.fold_in(rng, axis), (), 0, length) for axis, length in enumerate(array.shape)]
        where[longest] = (where[longest] + shift) % array.shape[longest]
        spots.append(tuple(where))
    return array.at[spots[0]].set(low).at[spots[1]].set(largest)


def levels(own_key, shape, pieces, least, high):
    factor_of, own = 1.0, jax.random.fold_in(own_key, 6)
    for axis_at, blocks in pieces:
        steps = jnp.exp(jax.random.uniform(jax.random.fold_in(own, axis_at), (blocks,), jnp.float32, least / len(pieces), high / len(pieces)))
        factor_of = factor_of * jnp.repeat(steps, shape[axis_at] // blocks).reshape([-1 if axis == axis_at else 1 for axis in range(len(shape))])
    return factor_of


def gaussian(rng, dims, width, most, shards=(), held_as=jnp.bfloat16):
    values = jax.random.normal(rng, dims, jnp.float32) * width
    if len(shards) > 0:
        values = levels(rng, dims, shards, -0.22, 0.18) * values
    return jnp.clip(values, min=-most, max=most).astype(held_as)


def setup_inputs(seed: int = 0) -> dict:
    key_of = jax.random.split(jax.random.key(seed), 4)
    return {
        "bands": gaussian(key_of[0], (BANDS, 4, NZ, NX, NY), 1.0, 6.0, ((0, 2), (2, 16))),
        "occ_level": place_ends(jax.random.randint(key_of[1], (BANDS,), 1, 5), jax.random.fold_in(key_of[1], 1), 1, 4).astype(jnp.int32),
        "block_owner": jax.random.randint(key_of[2], (1,), 0, BANDS).astype(jnp.int32),
    }


jacobi_diagonal = 6.5

def relax_field(density):
    field = density / jacobi_diagonal
    for sweep_index in range(SWEEPS - 1):
        beside = jnp.roll(field, 1, -3) + jnp.roll(field, -1, -3)
        beside = beside + jnp.roll(field, 1, -2) + jnp.roll(field, -1, -2)
        beside = beside + jnp.roll(field, 1, -1) + jnp.roll(field, -1, -1)
        field = (density + beside) / jacobi_diagonal
    return field

def reference(bands, occ_level, block_owner):
    first = block_owner[0].astype(jnp.int32)
    group = first // RES_DEV
    offset = first % RES_DEV
    picks = group * RES_DEV + (offset + jnp.arange(BLOCK, dtype=jnp.int32)) % RES_DEV
    block = jnp.take(bands, picks.astype(jnp.int32), axis=0).astype(jnp.float32)

    def one_band(total, item):
        orbital, level = item
        orbital = orbital.astype(jnp.float32)
        dens_real = orbital[0] * block[:, 0] + orbital[1] * block[:, 1] + orbital[2] * block[:, 2] + orbital[3] * block[:, 3]
        dens_imag = orbital[0] * block[:, 1] - orbital[1] * block[:, 0] + orbital[2] * block[:, 3] - orbital[3] * block[:, 2]
        pot_real = relax_field(dens_real)
        pot_imag = relax_field(dens_imag)
        weight = level.astype(jnp.float32) * 0.25
        parts = []
        for spin in range(2):
            parts.append(orbital[2 * spin] * pot_real - orbital[2 * spin + 1] * pot_imag)
            parts.append(orbital[2 * spin] * pot_imag + orbital[2 * spin + 1] * pot_real)
        return (total + weight * jnp.stack(parts, axis=1), None)
    initial = jnp.zeros((BLOCK, 4) + bands.shape[2:], jnp.float32)
    total, unused = lax.scan(one_band, initial, (bands, occ_level))
    return -(1.0 / jnp.sqrt(jnp.float32(BANDS))) * total
```

```python
import functools
import math

import jax
import jax.numpy as jnp
from jax import lax
from jax.experimental import pallas as pl
from jax.experimental.pallas import tpu as pltpu
from jax.sharding import PartitionSpec as P

MESH = pl.DeviceIdType.MESH
jacobi_diagonal = 6.5
inverse = 1.0 / jacobi_diagonal
RIM = 8
PACK = 16


def beside(field):
    rows, lanes = field.shape
    in_x = pltpu.roll(field, 1, 0) + pltpu.roll(field, rows - 1, 0)
    return in_x + pltpu.roll(field, 1, 1) + pltpu.roll(field, lanes - 1, 1)


def kernel(
    n_space, n_band, bands_ref, occ_ref, owner_ref, out_ref,
    give, every, occ_give, occ_every, dens, dens_give, below, above,
    third, third_give, third_below, third_above,
    band_send, band_recv, occ_send, occ_recv,
    halo_send, halo_recv, third_send, third_recv,
):
    count, comps, planes, x_rows, lanes = bands_ref.shape
    rows = x_rows // n_band
    total = count * n_band
    groups = dens.shape[0]
    me = lax.axis_index("band")
    spot = lax.axis_index("space")
    up = lax.rem(spot + 1, n_space)
    down = lax.rem(spot + n_space - 1, n_space)

    barrier = pltpu.get_barrier_semaphore()
    for step in range(1, n_band):
        pl.semaphore_signal(
            barrier, inc=1, device_id={"band": lax.rem(me + step, n_band)}, device_id_type=MESH
        )
    for place in (up, down):
        pl.semaphore_signal(barrier, inc=1, device_id={"space": place}, device_id_type=MESH)
    pl.semaphore_wait(barrier, n_band + 1)

    def rows_of(part, band, comp, plane):
        start = pl.multiple_of(part * rows, PACK)
        after = pl.multiple_of(lax.rem(part * rows + rows, x_rows), PACK)
        before = pl.multiple_of(lax.rem(part * rows + x_rows - PACK, x_rows), PACK)
        own = bands_ref[band, comp, plane, pl.ds(start, rows)]
        rim = jnp.concatenate(
            [
                bands_ref[band, comp, plane, pl.ds(after, PACK)].astype(jnp.float32)[:RIM],
                bands_ref[band, comp, plane, pl.ds(before, PACK)].astype(jnp.float32)[RIM:],
            ],
            axis=0,
        ).astype(jnp.bfloat16)
        return own, rim

    for band in range(count):
        occ_give[band] = jnp.full(occ_give.shape[1:], occ_ref[band], jnp.int32)
    mine = pl.ds(me * count, count)

    def band_copies(step):
        target = {"band": lax.rem(me + step, n_band)}
        return (
            pltpu.make_async_remote_copy(
                src_ref=give.at[step - 1], dst_ref=every.at[mine],
                send_sem=band_send.at[step - 1], recv_sem=band_recv.at[step - 1],
                device_id=target, device_id_type=MESH,
            ),
            pltpu.make_async_remote_copy(
                src_ref=occ_give, dst_ref=occ_every.at[mine],
                send_sem=occ_send.at[step - 1], recv_sem=occ_recv.at[step - 1],
                device_id=target, device_id_type=MESH,
            ),
        )

    for step in range(1, n_band):
        part = lax.rem(me + step, n_band)
        for band in range(count):
            for comp in range(comps):
                for plane in range(planes):
                    own, rim = rows_of(part, band, comp, plane)
                    give[step - 1, band, comp, plane, 0:rows] = own
                    give[step - 1, band, comp, plane, rows : rows + PACK] = rim
        for copy in band_copies(step):
            copy.start()
    for band in range(count):
        occ_every[me * count + band] = occ_give[band]
        for comp in range(comps):
            for plane in range(planes):
                own, rim = rows_of(me, band, comp, plane)
                every[me * count + band, comp, plane, 0:rows] = own
                every[me * count + band, comp, plane, rows : rows + PACK] = rim
    for step in range(1, n_band):
        for copy in band_copies(step):
            copy.wait_recv()

    first = owner_ref[0]
    start = lax.div(first, count) * count
    offset = lax.rem(first, count)
    block = [start + lax.rem(offset + j, count) for j in range(count)]

    def halo_copies(group):
        return (
            pltpu.make_async_remote_copy(
                src_ref=dens_give.at[group, :, pl.ds(planes - 2, 2)], dst_ref=below.at[group],
                send_sem=halo_send.at[0, group], recv_sem=halo_recv.at[0, group],
                device_id={"space": up}, device_id_type=MESH,
            ),
            pltpu.make_async_remote_copy(
                src_ref=dens_give.at[group, :, pl.ds(0, 2)], dst_ref=above.at[group],
                send_sem=halo_send.at[1, group], recv_sem=halo_recv.at[1, group],
                device_id={"space": down}, device_id_type=MESH,
            ),
        )

    def third_copies(group):
        return (
            pltpu.make_async_remote_copy(
                src_ref=third_give.at[1, group], dst_ref=third_below.at[group],
                send_sem=third_send.at[0, group], recv_sem=third_recv.at[0, group],
                device_id={"space": up}, device_id_type=MESH,
            ),
            pltpu.make_async_remote_copy(
                src_ref=third_give.at[0, group], dst_ref=third_above.at[group],
                send_sem=third_send.at[1, group], recv_sem=third_recv.at[1, group],
                device_id={"space": down}, device_id_type=MESH,
            ),
        )

    def load(band, plane):
        return [every[band, comp, plane].astype(jnp.float32) for comp in range(comps)]

    def real_part(a, b):
        return a[0] * b[0] + a[1] * b[1] + a[2] * b[2] + a[3] * b[3]

    def imag_part(a, b):
        return a[0] * b[1] - a[1] * b[0] + a[2] * b[3] - a[3] * b[2]

    def keep(group, field, plane, value):
        dens[group, field, plane] = value
        dens_give[group, field, plane] = value.astype(jnp.bfloat16)

    for plane in range(planes):
        a, b = load(block[0], plane), load(block[1], plane)
        keep(0, 0, plane, real_part(a, a))
        keep(0, 1, plane, real_part(b, b))
        keep(0, 2, plane, real_part(a, b))
        keep(0, 3, plane, imag_part(a, b))
    for copy in halo_copies(0):
        copy.start()

    def other(group):
        return lax.rem(start + count - 1 + group, total)

    def densities(group, carry):
        band = other(group)
        for plane in range(planes):
            a = load(band, plane)
            for j in range(count):
                b = load(block[j], plane)
                keep(group, 2 * j, plane, real_part(a, b))
                keep(group, 2 * j + 1, plane, imag_part(a, b))
        for copy in halo_copies(group):
            copy.start()
        return carry

    lax.fori_loop(1, groups, densities, 0)

    def sweeps(group, carry):
        for copy in halo_copies(group):
            copy.wait_recv()

        def one(field, inner):
            d = [below[group, field, k].astype(jnp.float32) for k in range(2)]
            d += [dens[group, field, k] for k in range(planes)]
            d += [above[group, field, k].astype(jnp.float32) for k in range(2)]
            second = [
                d[k] + inverse * (d[k - 1] + d[k + 1] + beside(d[k]))
                for k in range(1, planes + 3)
            ]
            for k in range(planes):
                value = d[k + 2] + inverse * (second[k] + second[k + 2] + beside(second[k + 1]))
                third[group, field, k] = value
                if k == 0:
                    third_give[0, group, field] = value[:rows].astype(jnp.bfloat16)
                if k == planes - 1:
                    third_give[1, group, field] = value[:rows].astype(jnp.bfloat16)
            return inner

        lax.fori_loop(0, dens.shape[1], one, 0)
        for copy in third_copies(group):
            copy.start()
        return carry

    lax.fori_loop(0, groups, sweeps, 0)

    def potential(group, field, plane):
        here = third[group, field, plane]
        if plane == 0:
            low = third_below[group, field].astype(jnp.float32)
        else:
            low = third[group, field, plane - 1, 0:rows]
        if plane == planes - 1:
            high = third_above[group, field].astype(jnp.float32)
        else:
            high = third[group, field, plane + 1, 0:rows]
        return dens[group, field, plane, 0:rows] + inverse * (low + high + beside(here)[:rows])

    scale = -inverse * 0.25 / math.sqrt(total)

    def orbital(band, plane):
        weight = occ_every[band, 0:1].astype(jnp.float32) * scale
        return [every[band, comp, plane, 0:rows].astype(jnp.float32) * weight for comp in range(comps)]

    def times(a, real, imag):
        parts = []
        for s in range(2):
            if imag is None:
                parts += [a[2 * s] * real, a[2 * s + 1] * real]
            else:
                parts += [a[2 * s] * real - a[2 * s + 1] * imag, a[2 * s] * imag + a[2 * s + 1] * real]
        return parts

    for copy in third_copies(0):
        copy.wait_recv()
    for plane in range(planes):
        a, b = orbital(block[0], plane), orbital(block[1], plane)
        real, imag = potential(0, 2, plane), potential(0, 3, plane)
        for j, (same, cross, sign) in enumerate(((a, b, -1.0), (b, a, 1.0))):
            one = times(same, potential(0, j, plane), None)
            two = times(cross, real, sign * imag)
            for comp in range(comps):
                out_ref[j, comp, plane] = one[comp] + two[comp]

    def finish(group, carry):
        for copy in third_copies(group):
            copy.wait_recv()
        band = other(group)
        for plane in range(planes):
            a = orbital(band, plane)
            for j in range(count):
                real, imag = potential(group, 2 * j, plane), potential(group, 2 * j + 1, plane)
                part = times(a, real, imag)
                for comp in range(comps):
                    out_ref[j, comp, plane] += part[comp]
        return carry

    lax.fori_loop(1, groups, finish, 0)

    for step in range(1, n_band):
        for copy in band_copies(step):
            copy.wait_send()

    def drain(group, carry):
        for copy in halo_copies(group) + third_copies(group):
            copy.wait_send()
        return carry

    lax.fori_loop(0, groups, drain, 0)


def on_device(n_space, n_band, bands, occ_level, block_owner):
    count, comps, planes, x_rows, lanes = bands.shape
    rows = x_rows // n_band
    ext = rows + PACK
    total = count * n_band
    groups = total - count + 1
    fields = 2 * count
    peers = max(n_band - 1, 1)
    assert count == 2 and comps == 4 and planes >= 2 and rows % PACK == 0
    half, full = jnp.bfloat16, jnp.float32
    return pl.pallas_call(
        functools.partial(kernel, n_space, n_band),
        out_shape=jax.ShapeDtypeStruct((count, comps, planes, rows, lanes), full),
        in_specs=[
            pl.BlockSpec(memory_space=pltpu.VMEM),
            pl.BlockSpec(memory_space=pltpu.SMEM),
            pl.BlockSpec(memory_space=pltpu.SMEM),
        ],
        out_specs=pl.BlockSpec(memory_space=pltpu.VMEM),
        scratch_shapes=[
            pltpu.VMEM((peers, count, comps, planes, ext, lanes), half),
            pltpu.VMEM((total, comps, planes, ext, lanes), half),
            pltpu.VMEM((count, 8, lanes), jnp.int32),
            pltpu.VMEM((total, 8, lanes), jnp.int32),
            pltpu.VMEM((groups, fields, planes, ext, lanes), full),
            pltpu.VMEM((groups, fields, planes, ext, lanes), half),
            pltpu.VMEM((groups, fields, 2, ext, lanes), half),
            pltpu.VMEM((groups, fields, 2, ext, lanes), half),
            pltpu.VMEM((groups, fields, planes, ext, lanes), full),
            pltpu.VMEM((2, groups, fields, rows, lanes), half),
            pltpu.VMEM((groups, fields, rows, lanes), half),
            pltpu.VMEM((groups, fields, rows, lanes), half),
            pltpu.SemaphoreType.DMA((peers,)),
            pltpu.SemaphoreType.DMA((peers,)),
            pltpu.SemaphoreType.DMA((peers,)),
            pltpu.SemaphoreType.DMA((peers,)),
            pltpu.SemaphoreType.DMA((2, groups)),
            pltpu.SemaphoreType.DMA((2, groups)),
            pltpu.SemaphoreType.DMA((2, groups)),
            pltpu.SemaphoreType.DMA((2, groups)),
        ],
        compiler_params=pltpu.CompilerParams(
            collective_id=0, has_side_effects=True, vmem_limit_bytes=48 * 1024 * 1024
        ),
    )(bands, occ_level, block_owner)


def solution(mesh):
    return jax.shard_map(
        functools.partial(on_device, mesh.shape["space"], mesh.shape["band"]),
        mesh=mesh,
        in_specs=(P("band", None, "space", None, None), P("band"), P()),
        out_specs=P(None, None, "space", "band", None),
        check_vma=False,
    )
```

```python
import functools
import math

import jax
import jax.numpy as jnp
from jax import lax
from jax.experimental import pallas as pl
from jax.experimental.pallas import tpu as pltpu
from jax.sharding import PartitionSpec as P

MESH = pl.DeviceIdType.MESH
jacobi_diagonal = 6.5
inverse = 1.0 / jacobi_diagonal
RIM = 8
PACK = 16


def beside(field):
    rows, lanes = field.shape
    in_x = pltpu.roll(field, 1, 0) + pltpu.roll(field, rows - 1, 0)
    return in_x + pltpu.roll(field, 1, 1) + pltpu.roll(field, lanes - 1, 1)


def kernel(
    n_space, n_band, bands_ref, occ_ref, owner_ref, out_ref,
    raw, rim_give, every, every_rim, occ_give, occ_every,
    dens, dens_give, dens_rim, below, above, below_rim, above_rim,
    third, third_give, third_below, third_above,
    local_sem, own_sem, band_send, band_recv, rim_send, rim_recv, occ_send, occ_recv,
    halo_send, halo_recv, edge_send, edge_recv, third_send, third_recv,
):
    count, comps, planes, x_rows, lanes = bands_ref.shape
    rows = x_rows // n_band
    chunks = rows // PACK
    total = count * n_band
    groups, fields = dens.shape[0], dens.shape[1]
    me = lax.axis_index("band")
    spot = lax.axis_index("space")
    up = lax.rem(spot + 1, n_space)
    down = lax.rem(spot + n_space - 1, n_space)
    mine = pl.ds(me * count, count)

    barrier = pltpu.get_barrier_semaphore()
    for step in range(1, n_band):
        pl.semaphore_signal(
            barrier, inc=1, device_id={"band": lax.rem(me + step, n_band)}, device_id_type=MESH
        )
    for place in (up, down):
        pl.semaphore_signal(barrier, inc=1, device_id={"space": place}, device_id_type=MESH)

    def local_copies(step):
        part = lax.rem(me + step, n_band)
        after = pl.multiple_of(lax.rem(part * rows + rows, x_rows), PACK)
        before = pl.multiple_of(lax.rem(part * rows + x_rows - PACK, x_rows), PACK)
        return [
            pltpu.make_async_copy(
                bands_ref.at[:, :, :, pl.ds(begin, PACK)], raw.at[step, side], local_sem.at[step, side]
            )
            for side, begin in enumerate((after, before))
        ]

    own_copies = [
        pltpu.make_async_copy(
            bands_ref.at[:, :, :, pl.ds(pl.multiple_of(me * rows + chunk * PACK, PACK), PACK)],
            every[chunk].at[mine],
            own_sem.at[chunk],
        )
        for chunk in range(chunks)
    ]
    for step in range(n_band):
        for copy in local_copies(step):
            copy.start()
    for copy in own_copies:
        copy.start()
    for band in range(count):
        occ_give[band] = jnp.full(occ_give.shape[1:], occ_ref[band], jnp.int32)
        occ_every[me * count + band] = jnp.full(occ_give.shape[1:], occ_ref[band], jnp.int32)

    pl.semaphore_wait(barrier, n_band + 1)

    def band_copy(step, chunk):
        part = lax.rem(me + step, n_band)
        return pltpu.make_async_remote_copy(
            src_ref=bands_ref.at[:, :, :, pl.ds(pl.multiple_of(part * rows + chunk * PACK, PACK), PACK)],
            dst_ref=every[chunk].at[mine],
            send_sem=band_send.at[step - 1, chunk], recv_sem=band_recv.at[step - 1, chunk],
            device_id={"band": part}, device_id_type=MESH,
        )

    def rim_copies(step):
        target = {"band": lax.rem(me + step, n_band)}
        return (
            pltpu.make_async_remote_copy(
                src_ref=rim_give.at[step - 1], dst_ref=every_rim.at[mine],
                send_sem=rim_send.at[step - 1], recv_sem=rim_recv.at[step - 1],
                device_id=target, device_id_type=MESH,
            ),
            pltpu.make_async_remote_copy(
                src_ref=occ_give, dst_ref=occ_every.at[mine],
                send_sem=occ_send.at[step - 1], recv_sem=occ_recv.at[step - 1],
                device_id=target, device_id_type=MESH,
            ),
        )

    for chunk in range(chunks):
        for step in range(1, n_band):
            band_copy(step, chunk).start()

    from_after = lax.broadcasted_iota(jnp.int32, (RIM, lanes), 0) < RIM // 2

    def packed_rim(step, band, comp):
        pieces = []
        for plane in range(planes):
            after = raw[step, 0, band, comp, plane].astype(jnp.float32)[:RIM]
            before = raw[step, 1, band, comp, plane].astype(jnp.float32)[RIM:]
            pieces.append(jnp.where(from_after, after, before))
        return jnp.concatenate(pieces, axis=0).astype(jnp.bfloat16)

    for step in range(n_band):
        for copy in local_copies(step):
            copy.wait()
    for step in range(1, n_band):
        for band in range(count):
            for comp in range(comps):
                rim_give[step - 1, band, comp] = packed_rim(step, band, comp)
        for copy in rim_copies(step):
            copy.start()
    for band in range(count):
        for comp in range(comps):
            every_rim[me * count + band, comp] = packed_rim(0, band, comp)
    for copy in own_copies:
        copy.wait()

    first = owner_ref[0]
    start = lax.div(first, count) * count
    offset = lax.rem(first, count)
    block = [start + lax.rem(offset + j, count) for j in range(count)]

    def halo_copies(group, chunk):
        return [
            pltpu.make_async_remote_copy(
                src_ref=dens_give.at[group, :, :, pl.ds(chunk * PACK, PACK)],
                dst_ref=landing.at[group, :, :, pl.ds(chunk * PACK, PACK)],
                send_sem=halo_send.at[way, group, chunk], recv_sem=halo_recv.at[way, group, chunk],
                device_id={"space": place}, device_id_type=MESH,
            )
            for way, (place, landing) in enumerate(((up, below), (down, above)))
        ]

    def edge_copies(group):
        return [
            pltpu.make_async_remote_copy(
                src_ref=dens_rim.at[group], dst_ref=landing.at[group],
                send_sem=edge_send.at[way, group], recv_sem=edge_recv.at[way, group],
                device_id={"space": place}, device_id_type=MESH,
            )
            for way, (place, landing) in enumerate(((up, below_rim), (down, above_rim)))
        ]

    def third_copies(group):
        return [
            pltpu.make_async_remote_copy(
                src_ref=third_give.at[1 - way, group], dst_ref=landing.at[group],
                send_sem=third_send.at[way, group], recv_sem=third_recv.at[way, group],
                device_id={"space": place}, device_id_type=MESH,
            )
            for way, (place, landing) in enumerate(((up, third_below), (down, third_above)))
        ]

    def real_part(a, b):
        return a[0] * b[0] + a[1] * b[1] + a[2] * b[2] + a[3] * b[3]

    def imag_part(a, b):
        return a[0] * b[1] - a[1] * b[0] + a[2] * b[3] - a[3] * b[2]

    def other(group):
        return lax.rem(start + count - 1 + group, total)

    def pair_fields(load, keep, sent):
        a, b = load(block[0]), load(block[1])
        keep(0, 0, real_part(a, a))
        keep(0, 1, real_part(b, b))
        keep(0, 2, real_part(a, b))
        keep(0, 3, imag_part(a, b))
        sent(0)

        def densities(group, carry):
            c = load(other(group))
            for j in range(count):
                right = load(block[j])
                keep(group, 2 * j, real_part(c, right))
                keep(group, 2 * j + 1, imag_part(c, right))
            sent(group)
            return carry

        lax.fori_loop(1, groups, densities, 0)

    for chunk in range(chunks):
        for step in range(1, n_band):
            band_copy(step, chunk).wait_recv()
        span = slice(chunk * PACK, chunk * PACK + PACK)

        def load(band):
            return [
                every[chunk][band, comp].astype(jnp.float32).reshape(planes * PACK, lanes)
                for comp in range(comps)
            ]

        def keep(group, field, value):
            for plane in range(planes):
                piece = value[plane * PACK : plane * PACK + PACK]
                dens[group, field, plane, span] = piece
                dens_give[group, field, plane, span] = piece.astype(jnp.bfloat16)

        def sent(group):
            for copy in halo_copies(group, chunk):
                copy.start()

        pair_fields(load, keep, sent)

    for step in range(1, n_band):
        for copy in rim_copies(step):
            copy.wait_recv()

    def load_rim(band):
        return [every_rim[band, comp].astype(jnp.float32) for comp in range(comps)]

    def keep_rim(group, field, value):
        dens_rim[group, field] = value.astype(jnp.bfloat16)
        for plane in range(planes):
            dens[group, field, plane, rows : rows + RIM] = value[plane * RIM : plane * RIM + RIM]

    def sent_rim(group):
        for copy in edge_copies(group):
            copy.start()

    pair_fields(load_rim, keep_rim, sent_rim)

    def sweeps(group, carry):
        for chunk in range(chunks):
            for copy in halo_copies(group, chunk):
                copy.wait_recv()
        for copy in edge_copies(group):
            copy.wait_recv()

        def one(field, inner):
            def landed(main, rim):
                edge = rim[group, field].astype(jnp.float32)
                return [
                    jnp.concatenate(
                        [main[group, field, k].astype(jnp.float32), edge[k * RIM : k * RIM + RIM]], axis=0
                    )
                    for k in range(planes)
                ]

            d = landed(below, below_rim)
            d += [dens[group, field, k] for k in range(planes)]
            d += landed(above, above_rim)
            second = [
                d[k] + inverse * (d[k - 1] + d[k + 1] + beside(d[k]))
                for k in range(1, planes + 3)
            ]
            for k in range(planes):
                value = d[k + 2] + inverse * (second[k] + second[k + 2] + beside(second[k + 1]))
                third[group, field, k] = value
                if k == 0:
                    third_give[0, group, field] = value[:rows].astype(jnp.bfloat16)
                if k == planes - 1:
                    third_give[1, group, field] = value[:rows].astype(jnp.bfloat16)
            return inner

        lax.fori_loop(0, fields, one, 0)
        for copy in third_copies(group):
            copy.start()
        return carry

    lax.fori_loop(0, groups, sweeps, 0)

    def potential(group, field, plane):
        here = third[group, field, plane]
        if plane == 0:
            low = third_below[group, field].astype(jnp.float32)
        else:
            low = third[group, field, plane - 1, 0:rows]
        if plane == planes - 1:
            high = third_above[group, field].astype(jnp.float32)
        else:
            high = third[group, field, plane + 1, 0:rows]
        return dens[group, field, plane, 0:rows] + inverse * (low + high + beside(here)[:rows])

    scale = -inverse * 0.25 / math.sqrt(total)

    def orbital(band, plane):
        weight = occ_every[band, 0:1].astype(jnp.float32) * scale
        return [
            jnp.concatenate([part[band, comp, plane].astype(jnp.float32) for part in every], axis=0) * weight
            for comp in range(comps)
        ]

    def times(a, real, imag):
        parts = []
        for s in range(2):
            if imag is None:
                parts += [a[2 * s] * real, a[2 * s + 1] * real]
            else:
                parts += [a[2 * s] * real - a[2 * s + 1] * imag, a[2 * s] * imag + a[2 * s + 1] * real]
        return parts

    for copy in third_copies(0):
        copy.wait_recv()
    for plane in range(planes):
        a, b = orbital(block[0], plane), orbital(block[1], plane)
        real, imag = potential(0, 2, plane), potential(0, 3, plane)
        for j, (same, cross, sign) in enumerate(((a, b, -1.0), (b, a, 1.0))):
            one = times(same, potential(0, j, plane), None)
            two = times(cross, real, sign * imag)
            for comp in range(comps):
                out_ref[j, comp, plane] = one[comp] + two[comp]

    def finish(group, carry):
        for copy in third_copies(group):
            copy.wait_recv()
        band = other(group)
        for plane in range(planes):
            a = orbital(band, plane)
            for j in range(count):
                real, imag = potential(group, 2 * j, plane), potential(group, 2 * j + 1, plane)
                part = times(a, real, imag)
                for comp in range(comps):
                    out_ref[j, comp, plane] += part[comp]
        return carry

    lax.fori_loop(1, groups, finish, 0)

    for step in range(1, n_band):
        for chunk in range(chunks):
            band_copy(step, chunk).wait_send()
        for copy in rim_copies(step):
            copy.wait_send()

    def drain(group, carry):
        for chunk in range(chunks):
            for copy in halo_copies(group, chunk):
                copy.wait_send()
        for copy in edge_copies(group) + third_copies(group):
            copy.wait_send()
        return carry

    lax.fori_loop(0, groups, drain, 0)


def on_device(n_space, n_band, bands, occ_level, block_owner):
    count, comps, planes, x_rows, lanes = bands.shape
    rows = x_rows // n_band
    chunks = rows // PACK
    ext = rows + RIM
    total = count * n_band
    groups = total - count + 1
    fields = 2 * count
    peers = max(n_band - 1, 1)
    assert count == 2 and comps == 4 and planes * RIM == PACK and rows % PACK == 0
    half, full, dma = jnp.bfloat16, jnp.float32, pltpu.SemaphoreType.DMA
    return pl.pallas_call(
        functools.partial(kernel, n_space, n_band),
        out_shape=jax.ShapeDtypeStruct((count, comps, planes, rows, lanes), full),
        in_specs=[
            pl.BlockSpec(memory_space=pl.ANY),
            pl.BlockSpec(memory_space=pltpu.SMEM),
            pl.BlockSpec(memory_space=pltpu.SMEM),
        ],
        out_specs=pl.BlockSpec(memory_space=pltpu.VMEM),
        scratch_shapes=[
            pltpu.VMEM((n_band, 2, count, comps, planes, PACK, lanes), half),
            pltpu.VMEM((peers, count, comps, PACK, lanes), half),
            [pltpu.VMEM((total, comps, planes, PACK, lanes), half) for chunk in range(chunks)],
            pltpu.VMEM((total, comps, PACK, lanes), half),
            pltpu.VMEM((count, 8, lanes), jnp.int32),
            pltpu.VMEM((total, 8, lanes), jnp.int32),
            pltpu.VMEM((groups, fields, planes, ext, lanes), full),
            pltpu.VMEM((groups, fields, planes, rows, lanes), half),
            pltpu.VMEM((groups, fields, PACK, lanes), half),
            pltpu.VMEM((groups, fields, planes, rows, lanes), half),
            pltpu.VMEM((groups, fields, planes, rows, lanes), half),
            pltpu.VMEM((groups, fields, PACK, lanes), half),
            pltpu.VMEM((groups, fields, PACK, lanes), half),
            pltpu.VMEM((groups, fields, planes, ext, lanes), full),
            pltpu.VMEM((2, groups, fields, rows, lanes), half),
            pltpu.VMEM((groups, fields, rows, lanes), half),
            pltpu.VMEM((groups, fields, rows, lanes), half),
            dma((n_band, 2)),
            dma((chunks,)),
            dma((peers, chunks)),
            dma((peers, chunks)),
            dma((peers,)),
            dma((peers,)),
            dma((peers,)),
            dma((peers,)),
            dma((2, groups, chunks)),
            dma((2, groups, chunks)),
            dma((2, groups)),
            dma((2, groups)),
            dma((2, groups)),
            dma((2, groups)),
        ],
        compiler_params=pltpu.CompilerParams(
            collective_id=0, has_side_effects=True, vmem_limit_bytes=48 * 1024 * 1024
        ),
    )(bands, occ_level, block_owner)


def solution(mesh):
    return jax.shard_map(
        functools.partial(on_device, mesh.shape["space"], mesh.shape["band"]),
        mesh=mesh,
        in_specs=(P("band", None, "space", None, None), P("band"), P()),
        out_specs=P(None, None, "space", "band", None),
        check_vma=False,
    )
```

```python
import functools
import math

import jax
import jax.numpy as jnp
from jax import lax
from jax.experimental import pallas as pl
from jax.experimental.pallas import tpu as pltpu
from jax.sharding import PartitionSpec as P

MESH = pl.DeviceIdType.MESH
jacobi_diagonal = 6.5
inverse = 1.0 / jacobi_diagonal
RIM = 8
PACK = 16


def beside(field):
    rows, lanes = field.shape
    in_x = pltpu.roll(field, 1, 0) + pltpu.roll(field, rows - 1, 0)
    return in_x + pltpu.roll(field, 1, 1) + pltpu.roll(field, lanes - 1, 1)


def kernel(
    n_space, n_band, bands_ref, occ_hbm, owner_hbm, out_hbm,
    occ_ref, owner_ref, out_ref, scalar_sem, out_sem,
    raw, rim_give, every, every_rim, occ_give, occ_every,
    dens, dens_give, dens_rim, below, above, below_rim, above_rim,
    third, third_give, third_below, third_above,
    local_sem, own_sem, band_send, band_recv, rim_send, rim_recv, occ_send, occ_recv,
    halo_send, halo_recv, edge_send, edge_recv, third_send, third_recv,
):
    count, comps, planes, x_rows, lanes = bands_ref.shape
    rows = x_rows // n_band
    chunks = rows // PACK
    total = count * n_band
    groups, fields = dens.shape[0], dens.shape[1]
    me = lax.axis_index("band")
    spot = lax.axis_index("space")
    up = lax.rem(spot + 1, n_space)
    down = lax.rem(spot + n_space - 1, n_space)
    mine = pl.ds(me * count, count)

    barrier = pltpu.get_barrier_semaphore()
    for step in range(1, n_band):
        pl.semaphore_signal(
            barrier, inc=1, device_id={"band": lax.rem(me + step, n_band)}, device_id_type=MESH
        )
    for place in (up, down):
        pl.semaphore_signal(barrier, inc=1, device_id={"space": place}, device_id_type=MESH)

    def local_copies(step):
        part = lax.rem(me + step, n_band)
        after = pl.multiple_of(lax.rem(part * rows + rows, x_rows), PACK)
        before = pl.multiple_of(lax.rem(part * rows + x_rows - PACK, x_rows), PACK)
        return [
            pltpu.make_async_copy(
                bands_ref.at[:, :, :, pl.ds(begin, PACK)], raw.at[step, side], local_sem.at[step, side]
            )
            for side, begin in enumerate((after, before))
        ]

    own_copies = [
        pltpu.make_async_copy(
            bands_ref.at[:, :, :, pl.ds(pl.multiple_of(me * rows + chunk * PACK, PACK), PACK)],
            every[chunk].at[mine],
            own_sem.at[chunk],
        )
        for chunk in range(chunks)
    ]
    for step in range(n_band):
        for copy in local_copies(step):
            copy.start()
    for copy in own_copies:
        copy.start()
    scalars = [
        pltpu.make_async_copy(occ_hbm, occ_ref, scalar_sem.at[0]),
        pltpu.make_async_copy(owner_hbm, owner_ref, scalar_sem.at[1]),
    ]
    for copy in scalars:
        copy.start()
    pl.semaphore_wait(barrier, n_band + 1)

    def band_copy(step, chunk):
        part = lax.rem(me + step, n_band)
        return pltpu.make_async_remote_copy(
            src_ref=bands_ref.at[:, :, :, pl.ds(pl.multiple_of(part * rows + chunk * PACK, PACK), PACK)],
            dst_ref=every[chunk].at[mine],
            send_sem=band_send.at[step - 1, chunk], recv_sem=band_recv.at[step - 1, chunk],
            device_id={"band": part}, device_id_type=MESH,
        )

    def rim_copies(step):
        target = {"band": lax.rem(me + step, n_band)}
        return (
            pltpu.make_async_remote_copy(
                src_ref=rim_give.at[step - 1], dst_ref=every_rim.at[mine],
                send_sem=rim_send.at[step - 1], recv_sem=rim_recv.at[step - 1],
                device_id=target, device_id_type=MESH,
            ),
            pltpu.make_async_remote_copy(
                src_ref=occ_give, dst_ref=occ_every.at[mine],
                send_sem=occ_send.at[step - 1], recv_sem=occ_recv.at[step - 1],
                device_id=target, device_id_type=MESH,
            ),
        )

    late = min(2, chunks)
    early = chunks - late
    for chunk in range(early):
        for step in range(1, n_band):
            band_copy(step, chunk).start()

    from_after = lax.broadcasted_iota(jnp.int32, (RIM, lanes), 0) < RIM // 2

    def packed_rim(step, band, comp):
        pieces = []
        for plane in range(planes):
            after = raw[step, 0, band, comp, plane].astype(jnp.float32)[:RIM]
            before = raw[step, 1, band, comp, plane].astype(jnp.float32)[RIM:]
            pieces.append(jnp.where(from_after, after, before))
        return jnp.concatenate(pieces, axis=0).astype(jnp.bfloat16)

    for step in range(n_band):
        for copy in local_copies(step):
            copy.wait()
    for copy in scalars:
        copy.wait()
    for band in range(count):
        occ_give[band] = jnp.full(occ_give.shape[1:], occ_ref[band], jnp.int32)
        occ_every[me * count + band] = jnp.full(occ_give.shape[1:], occ_ref[band], jnp.int32)
    for step in range(1, n_band):
        for band in range(count):
            for comp in range(comps):
                rim_give[step - 1, band, comp] = packed_rim(step, band, comp)
        for copy in rim_copies(step):
            copy.start()
    for chunk in range(early, chunks):
        for step in range(1, n_band):
            band_copy(step, chunk).start()
    for band in range(count):
        for comp in range(comps):
            every_rim[me * count + band, comp] = packed_rim(0, band, comp)
    for copy in own_copies:
        copy.wait()

    first = owner_ref[0]
    start = lax.div(first, count) * count
    offset = lax.rem(first, count)
    block = [start + lax.rem(offset + j, count) for j in range(count)]

    def halo_copies(group, chunk):
        return [
            pltpu.make_async_remote_copy(
                src_ref=dens_give.at[group, :, :, pl.ds(chunk * PACK, PACK)],
                dst_ref=landing.at[group, :, :, pl.ds(chunk * PACK, PACK)],
                send_sem=halo_send.at[way, group, chunk], recv_sem=halo_recv.at[way, group, chunk],
                device_id={"space": place}, device_id_type=MESH,
            )
            for way, (place, landing) in enumerate(((up, below), (down, above)))
        ]

    def edge_copies(group):
        return [
            pltpu.make_async_remote_copy(
                src_ref=dens_rim.at[group], dst_ref=landing.at[group],
                send_sem=edge_send.at[way, group], recv_sem=edge_recv.at[way, group],
                device_id={"space": place}, device_id_type=MESH,
            )
            for way, (place, landing) in enumerate(((up, below_rim), (down, above_rim)))
        ]

    def third_copies(group):
        return [
            pltpu.make_async_remote_copy(
                src_ref=third_give.at[1 - way, group], dst_ref=landing.at[group],
                send_sem=third_send.at[way, group], recv_sem=third_recv.at[way, group],
                device_id={"space": place}, device_id_type=MESH,
            )
            for way, (place, landing) in enumerate(((up, third_below), (down, third_above)))
        ]

    def real_part(a, b):
        return a[0] * b[0] + a[1] * b[1] + a[2] * b[2] + a[3] * b[3]

    def imag_part(a, b):
        return a[0] * b[1] - a[1] * b[0] + a[2] * b[3] - a[3] * b[2]

    def other(group):
        return lax.rem(start + count - 1 + group, total)

    def block_fields(load, keep):
        a, b = load(block[0]), load(block[1])
        keep(0, 0, real_part(a, a))
        keep(0, 1, real_part(b, b))
        keep(0, 2, real_part(a, b))
        keep(0, 3, imag_part(a, b))

    def other_fields(group, load, keep):
        c = load(other(group))
        for j in range(count):
            right = load(block[j])
            keep(group, 2 * j, real_part(c, right))
            keep(group, 2 * j + 1, imag_part(c, right))

    def chunk_io(chunk):
        span = slice(chunk * PACK, chunk * PACK + PACK)

        def load(band):
            return [
                every[chunk][band, comp].astype(jnp.float32).reshape(planes * PACK, lanes)
                for comp in range(comps)
            ]

        def keep(group, field, value):
            for plane in range(planes):
                piece = value[plane * PACK : plane * PACK + PACK]
                dens[group, field, plane, span] = piece
                dens_give[group, field, plane, span] = piece.astype(jnp.bfloat16)

        return load, keep, lambda group: halo_copies(group, chunk)

    def load_rim(band):
        return [every_rim[band, comp].astype(jnp.float32) for comp in range(comps)]

    def keep_rim(group, field, value):
        dens_rim[group, field] = value.astype(jnp.bfloat16)
        for plane in range(planes):
            dens[group, field, plane, rows : rows + RIM] = value[plane * RIM : plane * RIM + RIM]

    def stage(pieces):
        for load, keep, copies in pieces:
            block_fields(load, keep)
            for copy in copies(0):
                copy.start()

        def densities(group, carry):
            for load, keep, copies in pieces:
                other_fields(group, load, keep)
                for copy in copies(group):
                    copy.start()
            return carry

        lax.fori_loop(1, groups, densities, 0)

    for chunk in range(early):
        for step in range(1, n_band):
            band_copy(step, chunk).wait_recv()
        stage([chunk_io(chunk)])
    for step in range(1, n_band):
        for copy in rim_copies(step):
            copy.wait_recv()
    stage([(load_rim, keep_rim, edge_copies)])
    for chunk in range(early, chunks):
        for step in range(1, n_band):
            band_copy(step, chunk).wait_recv()
    stage([chunk_io(chunk) for chunk in range(early, chunks)])

    def sweeps(group, carry):
        for chunk in range(chunks):
            for copy in halo_copies(group, chunk):
                copy.wait_recv()
        for copy in edge_copies(group):
            copy.wait_recv()

        def one(field, inner):
            def landed(main, rim):
                edge = rim[group, field].astype(jnp.float32)
                return [
                    jnp.concatenate(
                        [main[group, field, k].astype(jnp.float32), edge[k * RIM : k * RIM + RIM]], axis=0
                    )
                    for k in range(planes)
                ]

            d = landed(below, below_rim)
            d += [dens[group, field, k] for k in range(planes)]
            d += landed(above, above_rim)
            second = [
                d[k] + inverse * (d[k - 1] + d[k + 1] + beside(d[k]))
                for k in range(1, planes + 3)
            ]
            for k in range(planes):
                value = d[k + 2] + inverse * (second[k] + second[k + 2] + beside(second[k + 1]))
                third[group, field, k] = value
                if k == 0:
                    third_give[0, group, field] = value[:rows].astype(jnp.bfloat16)
                if k == planes - 1:
                    third_give[1, group, field] = value[:rows].astype(jnp.bfloat16)
            return inner

        lax.fori_loop(0, fields, one, 0)
        for copy in third_copies(group):
            copy.start()
        return carry

    lax.fori_loop(0, groups, sweeps, 0)

    def potential(group, field, plane):
        here = third[group, field, plane]
        if plane == 0:
            low = third_below[group, field].astype(jnp.float32)
        else:
            low = third[group, field, plane - 1, 0:rows]
        if plane == planes - 1:
            high = third_above[group, field].astype(jnp.float32)
        else:
            high = third[group, field, plane + 1, 0:rows]
        return dens[group, field, plane, 0:rows] + inverse * (low + high + beside(here)[:rows])

    scale = -inverse * 0.25 / math.sqrt(total)

    def orbital(band, plane):
        weight = occ_every[band, 0:1].astype(jnp.float32) * scale
        return [
            jnp.concatenate([part[band, comp, plane].astype(jnp.float32) for part in every], axis=0) * weight
            for comp in range(comps)
        ]

    def times(a, real, imag):
        parts = []
        for s in range(2):
            if imag is None:
                parts += [a[2 * s] * real, a[2 * s + 1] * real]
            else:
                parts += [a[2 * s] * real - a[2 * s + 1] * imag, a[2 * s] * imag + a[2 * s + 1] * real]
        return parts

    for copy in third_copies(0):
        copy.wait_recv()
    for plane in range(planes):
        a, b = orbital(block[0], plane), orbital(block[1], plane)
        real, imag = potential(0, 2, plane), potential(0, 3, plane)
        for j, (same, cross, sign) in enumerate(((a, b, -1.0), (b, a, 1.0))):
            one = times(same, potential(0, j, plane), None)
            two = times(cross, real, sign * imag)
            for comp in range(comps):
                out_ref[plane, j, comp] = one[comp] + two[comp]

    def out_copy(plane):
        return pltpu.make_async_copy(out_ref.at[plane], out_hbm.at[:, :, plane], out_sem.at[plane])

    def finish(group, carry, last=False):
        for copy in third_copies(group):
            copy.wait_recv()
        band = other(group)
        for plane in range(planes):
            a = orbital(band, plane)
            for j in range(count):
                real, imag = potential(group, 2 * j, plane), potential(group, 2 * j + 1, plane)
                part = times(a, real, imag)
                for comp in range(comps):
                    out_ref[plane, j, comp] += part[comp]
            if last:
                out_copy(plane).start()
        return carry

    if groups > 1:
        lax.fori_loop(1, groups - 1, finish, 0)
        finish(groups - 1, 0, last=True)
    else:
        for plane in range(planes):
            out_copy(plane).start()

    for step in range(1, n_band):
        for chunk in range(chunks):
            band_copy(step, chunk).wait_send()
        for copy in rim_copies(step):
            copy.wait_send()

    def drain(group, carry):
        for chunk in range(chunks):
            for copy in halo_copies(group, chunk):
                copy.wait_send()
        for copy in edge_copies(group) + third_copies(group):
            copy.wait_send()
        return carry

    lax.fori_loop(0, groups, drain, 0)
    for plane in range(planes):
        out_copy(plane).wait()


def on_device(n_space, n_band, bands, occ_level, block_owner):
    count, comps, planes, x_rows, lanes = bands.shape
    rows = x_rows // n_band
    chunks = rows // PACK
    ext = rows + RIM
    total = count * n_band
    groups = total - count + 1
    fields = 2 * count
    peers = max(n_band - 1, 1)
    assert count == 2 and comps == 4 and planes * RIM == PACK and rows % PACK == 0
    half, full, dma = jnp.bfloat16, jnp.float32, pltpu.SemaphoreType.DMA
    return pl.pallas_call(
        functools.partial(kernel, n_space, n_band),
        out_shape=jax.ShapeDtypeStruct((count, comps, planes, rows, lanes), full),
        in_specs=[pl.BlockSpec(memory_space=pl.ANY)] * 3,
        out_specs=pl.BlockSpec(memory_space=pl.ANY),
        scratch_shapes=[
            pltpu.SMEM((count,), jnp.int32),
            pltpu.SMEM((1,), jnp.int32),
            pltpu.VMEM((planes, count, comps, rows, lanes), full),
            dma((2,)),
            dma((planes,)),
            pltpu.VMEM((n_band, 2, count, comps, planes, PACK, lanes), half),
            pltpu.VMEM((peers, count, comps, PACK, lanes), half),
            [pltpu.VMEM((total, comps, planes, PACK, lanes), half) for chunk in range(chunks)],
            pltpu.VMEM((total, comps, PACK, lanes), half),
            pltpu.VMEM((count, 8, lanes), jnp.int32),
            pltpu.VMEM((total, 8, lanes), jnp.int32),
            pltpu.VMEM((groups, fields, planes, ext, lanes), full),
            pltpu.VMEM((groups, fields, planes, rows, lanes), half),
            pltpu.VMEM((groups, fields, PACK, lanes), half),
            pltpu.VMEM((groups, fields, planes, rows, lanes), half),
            pltpu.VMEM((groups, fields, planes, rows, lanes), half),
            pltpu.VMEM((groups, fields, PACK, lanes), half),
            pltpu.VMEM((groups, fields, PACK, lanes), half),
            pltpu.VMEM((groups, fields, planes, ext, lanes), full),
            pltpu.VMEM((2, groups, fields, rows, lanes), half),
            pltpu.VMEM((groups, fields, rows, lanes), half),
            pltpu.VMEM((groups, fields, rows, lanes), half),
            dma((n_band, 2)),
            dma((chunks,)),
            dma((peers, chunks)),
            dma((peers, chunks)),
            dma((peers,)),
            dma((peers,)),
            dma((peers,)),
            dma((peers,)),
            dma((2, groups, chunks)),
            dma((2, groups, chunks)),
            dma((2, groups)),
            dma((2, groups)),
            dma((2, groups)),
            dma((2, groups)),
        ],
        compiler_params=pltpu.CompilerParams(
            collective_id=0, has_side_effects=True, vmem_limit_bytes=65280 * 1024
        ),
    )(bands, occ_level, block_owner)


def solution(mesh):
    return jax.shard_map(
        functools.partial(on_device, mesh.shape["space"], mesh.shape["band"]),
        mesh=mesh,
        in_specs=(P("band", None, "space", None, None), P("band"), P()),
        out_specs=P(None, None, "space", "band", None),
        check_vma=False,
    )
```

```python
import functools
import math

import jax
import jax.numpy as jnp
from jax import lax
from jax.experimental import pallas as pl
from jax.experimental.pallas import tpu as pltpu
from jax.sharding import PartitionSpec as P

MESH = pl.DeviceIdType.MESH
jacobi_diagonal = 6.5
inverse = 1.0 / jacobi_diagonal
RIM = 8
PACK = 16


def beside(field):
    rows, lanes = field.shape
    in_x = pltpu.roll(field, 1, 0) + pltpu.roll(field, rows - 1, 0)
    return in_x + pltpu.roll(field, 1, 1) + pltpu.roll(field, lanes - 1, 1)


def kernel(
    n_space, n_band, bands_ref, occ_hbm, owner_hbm, out_hbm,
    occ_ref, owner_ref, out_ref, scalar_sem, out_sem,
    raw, rim_give, every, every_rim, occ_give, occ_every,
    dens, dens_give, dens_rim, below, above, below_rim, above_rim,
    third, third_give, third_below, third_above,
    local_sem, own_sem, band_send, band_recv, rim_send, rim_recv, occ_send, occ_recv,
    halo_send, halo_recv, edge_send, edge_recv, third_send, third_recv,
):
    count, comps, planes, x_rows, lanes = bands_ref.shape
    rows = x_rows // n_band
    chunks = rows // PACK
    total = count * n_band
    groups, fields = dens.shape[0], dens.shape[1]
    me = lax.axis_index("band")
    spot = lax.axis_index("space")
    up = lax.rem(spot + 1, n_space)
    down = lax.rem(spot + n_space - 1, n_space)
    mine = pl.ds(me * count, count)

    barrier = pltpu.get_barrier_semaphore()
    for step in range(1, n_band):
        pl.semaphore_signal(
            barrier, inc=1, device_id={"band": lax.rem(me + step, n_band)}, device_id_type=MESH
        )
    for place in (up, down):
        pl.semaphore_signal(barrier, inc=1, device_id={"space": place}, device_id_type=MESH)

    def local_copies(step):
        part = lax.rem(me + step, n_band)
        after = pl.multiple_of(lax.rem(part * rows + rows, x_rows), PACK)
        before = pl.multiple_of(lax.rem(part * rows + x_rows - PACK, x_rows), PACK)
        return [
            pltpu.make_async_copy(
                bands_ref.at[:, :, :, pl.ds(begin, PACK)], raw.at[step, side], local_sem.at[step, side]
            )
            for side, begin in enumerate((after, before))
        ]

    own_copies = [
        pltpu.make_async_copy(
            bands_ref.at[:, :, :, pl.ds(pl.multiple_of(me * rows + chunk * PACK, PACK), PACK)],
            every[chunk].at[mine],
            own_sem.at[chunk],
        )
        for chunk in range(chunks)
    ]
    for step in range(n_band):
        for copy in local_copies(step):
            copy.start()
    for copy in own_copies:
        copy.start()
    scalars = [
        pltpu.make_async_copy(occ_hbm, occ_ref, scalar_sem.at[0]),
        pltpu.make_async_copy(owner_hbm, owner_ref, scalar_sem.at[1]),
    ]
    for copy in scalars:
        copy.start()
    pl.semaphore_wait(barrier, n_band + 1)

    def band_copy(step, chunk):
        part = lax.rem(me + step, n_band)
        return pltpu.make_async_remote_copy(
            src_ref=bands_ref.at[:, :, :, pl.ds(pl.multiple_of(part * rows + chunk * PACK, PACK), PACK)],
            dst_ref=every[chunk].at[mine],
            send_sem=band_send.at[step - 1, chunk], recv_sem=band_recv.at[step - 1, chunk],
            device_id={"band": part}, device_id_type=MESH,
        )

    def rim_copies(step):
        target = {"band": lax.rem(me + step, n_band)}
        return (
            pltpu.make_async_remote_copy(
                src_ref=rim_give.at[step - 1], dst_ref=every_rim.at[mine],
                send_sem=rim_send.at[step - 1], recv_sem=rim_recv.at[step - 1],
                device_id=target, device_id_type=MESH,
            ),
            pltpu.make_async_remote_copy(
                src_ref=occ_give, dst_ref=occ_every.at[mine],
                send_sem=occ_send.at[step - 1], recv_sem=occ_recv.at[step - 1],
                device_id=target, device_id_type=MESH,
            ),
        )

    late = min(2, chunks)
    early = chunks - late
    for chunk in range(early):
        for step in range(1, n_band):
            band_copy(step, chunk).start()

    from_after = lax.broadcasted_iota(jnp.int32, (RIM, lanes), 0) < RIM // 2

    def packed_rim(step, band, comp):
        pieces = []
        for plane in range(planes):
            after = raw[step, 0, band, comp, plane].astype(jnp.float32)[:RIM]
            before = raw[step, 1, band, comp, plane].astype(jnp.float32)[RIM:]
            pieces.append(jnp.where(from_after, after, before))
        return jnp.concatenate(pieces, axis=0).astype(jnp.bfloat16)

    for step in range(n_band):
        for copy in local_copies(step):
            copy.wait()
    for copy in scalars:
        copy.wait()
    for band in range(count):
        occ_give[band] = jnp.full(occ_give.shape[1:], occ_ref[band], jnp.int32)
        occ_every[me * count + band] = jnp.full(occ_give.shape[1:], occ_ref[band], jnp.int32)
    for step in range(1, n_band):
        for band in range(count):
            for comp in range(comps):
                rim_give[step - 1, band, comp] = packed_rim(step, band, comp)
        for copy in rim_copies(step):
            copy.start()
    for chunk in range(early, chunks):
        for step in range(1, n_band):
            band_copy(step, chunk).start()
    for band in range(count):
        for comp in range(comps):
            every_rim[me * count + band, comp] = packed_rim(0, band, comp)
    for copy in own_copies:
        copy.wait()

    first = owner_ref[0]
    start = lax.div(first, count) * count
    offset = lax.rem(first, count)
    block = [start + lax.rem(offset + j, count) for j in range(count)]

    def halo_copies(group, chunk):
        return [
            pltpu.make_async_remote_copy(
                src_ref=dens_give.at[group, :, :, pl.ds(chunk * PACK, PACK)],
                dst_ref=landing.at[group, :, :, pl.ds(chunk * PACK, PACK)],
                send_sem=halo_send.at[way, group, chunk], recv_sem=halo_recv.at[way, group, chunk],
                device_id={"space": place}, device_id_type=MESH,
            )
            for way, (place, landing) in enumerate(((up, below), (down, above)))
        ]

    def edge_copies(group):
        return [
            pltpu.make_async_remote_copy(
                src_ref=dens_rim.at[group], dst_ref=landing.at[group],
                send_sem=edge_send.at[way, group], recv_sem=edge_recv.at[way, group],
                device_id={"space": place}, device_id_type=MESH,
            )
            for way, (place, landing) in enumerate(((up, below_rim), (down, above_rim)))
        ]

    def third_copies(group, field):
        return [
            pltpu.make_async_remote_copy(
                src_ref=third_give.at[1 - way, group, field], dst_ref=landing.at[group, field],
                send_sem=third_send.at[way, group, field], recv_sem=third_recv.at[way, group, field],
                device_id={"space": place}, device_id_type=MESH,
            )
            for way, (place, landing) in enumerate(((up, third_below), (down, third_above)))
        ]

    def real_part(a, b):
        return a[0] * b[0] + a[1] * b[1] + a[2] * b[2] + a[3] * b[3]

    def imag_part(a, b):
        return a[0] * b[1] - a[1] * b[0] + a[2] * b[3] - a[3] * b[2]

    def other(group):
        return lax.rem(start + count - 1 + group, total)

    def block_fields(load, keep):
        a, b = load(block[0]), load(block[1])
        keep(0, 0, real_part(a, a))
        keep(0, 1, real_part(b, b))
        keep(0, 2, real_part(a, b))
        keep(0, 3, imag_part(a, b))

    def other_fields(group, load, keep):
        c = load(other(group))
        for j in range(count):
            right = load(block[j])
            keep(group, 2 * j, real_part(c, right))
            keep(group, 2 * j + 1, imag_part(c, right))

    def chunk_io(chunk):
        span = slice(chunk * PACK, chunk * PACK + PACK)

        def load(band):
            return [
                every[chunk][band, comp].astype(jnp.float32).reshape(planes * PACK, lanes)
                for comp in range(comps)
            ]

        def keep(group, field, value):
            for plane in range(planes):
                piece = value[plane * PACK : plane * PACK + PACK]
                dens[group, field, plane, span] = piece
                dens_give[group, field, plane, span] = piece.astype(jnp.bfloat16)

        return load, keep, lambda group: halo_copies(group, chunk)

    def load_rim(band):
        return [every_rim[band, comp].astype(jnp.float32) for comp in range(comps)]

    def keep_rim(group, field, value):
        dens_rim[group, field] = value.astype(jnp.bfloat16)
        for plane in range(planes):
            dens[group, field, plane, rows : rows + RIM] = value[plane * RIM : plane * RIM + RIM]

    def stage(pieces):
        for load, keep, copies in pieces:
            block_fields(load, keep)
            for copy in copies(0):
                copy.start()

        def densities(group, carry):
            for load, keep, copies in pieces:
                other_fields(group, load, keep)
                for copy in copies(group):
                    copy.start()
            return carry

        lax.fori_loop(1, groups, densities, 0)

    for chunk in range(early):
        for step in range(1, n_band):
            band_copy(step, chunk).wait_recv()
        stage([chunk_io(chunk)])
    for step in range(1, n_band):
        for copy in rim_copies(step):
            copy.wait_recv()
    stage([(load_rim, keep_rim, edge_copies)])
    for chunk in range(early, chunks):
        for step in range(1, n_band):
            band_copy(step, chunk).wait_recv()
    stage([chunk_io(chunk) for chunk in range(early, chunks)])

    def sweeps(group, carry):
        for chunk in range(chunks):
            for copy in halo_copies(group, chunk):
                copy.wait_recv()
        for copy in edge_copies(group):
            copy.wait_recv()

        def one(field, inner):
            def landed(main, rim):
                edge = rim[group, field].astype(jnp.float32)
                return [
                    jnp.concatenate(
                        [main[group, field, k].astype(jnp.float32), edge[k * RIM : k * RIM + RIM]], axis=0
                    )
                    for k in range(planes)
                ]

            d = landed(below, below_rim)
            d += [dens[group, field, k] for k in range(planes)]
            d += landed(above, above_rim)
            second = [
                d[k] + inverse * (d[k - 1] + d[k + 1] + beside(d[k]))
                for k in range(1, planes + 3)
            ]
            for k in range(planes):
                value = d[k + 2] + inverse * (second[k] + second[k + 2] + beside(second[k + 1]))
                third[group, field, k] = value
                if k == 0:
                    third_give[0, group, field] = value[:rows].astype(jnp.bfloat16)
                if k == planes - 1:
                    third_give[1, group, field] = value[:rows].astype(jnp.bfloat16)
            for copy in third_copies(group, field):
                copy.start()
            return inner

        lax.fori_loop(0, fields, one, 0)
        return carry

    lax.fori_loop(0, groups, sweeps, 0)

    def potential(group, field, plane):
        here = third[group, field, plane]
        if plane == 0:
            low = third_below[group, field].astype(jnp.float32)
        else:
            low = third[group, field, plane - 1, 0:rows]
        if plane == planes - 1:
            high = third_above[group, field].astype(jnp.float32)
        else:
            high = third[group, field, plane + 1, 0:rows]
        return dens[group, field, plane, 0:rows] + inverse * (low + high + beside(here)[:rows])

    scale = -inverse * 0.25 / math.sqrt(total)

    def orbital(band, plane):
        weight = occ_every[band, 0:1].astype(jnp.float32) * scale
        return [
            jnp.concatenate([part[band, comp, plane].astype(jnp.float32) for part in every], axis=0) * weight
            for comp in range(comps)
        ]

    def times(a, real, imag):
        parts = []
        for s in range(2):
            if imag is None:
                parts += [a[2 * s] * real, a[2 * s + 1] * real]
            else:
                parts += [a[2 * s] * real - a[2 * s + 1] * imag, a[2 * s] * imag + a[2 * s + 1] * real]
        return parts

    for field in range(fields):
        for copy in third_copies(0, field):
            copy.wait_recv()
    for plane in range(planes):
        a, b = orbital(block[0], plane), orbital(block[1], plane)
        real, imag = potential(0, 2, plane), potential(0, 3, plane)
        for j, (same, cross, sign) in enumerate(((a, b, -1.0), (b, a, 1.0))):
            one = times(same, potential(0, j, plane), None)
            two = times(cross, real, sign * imag)
            for comp in range(comps):
                out_ref[j, comp, plane] = one[comp] + two[comp]

    def out_copy(j):
        return pltpu.make_async_copy(out_ref.at[j], out_hbm.at[j], out_sem.at[j])

    def finish(group, carry, last=False):
        band = other(group)
        for j in range(count):
            for field in (2 * j, 2 * j + 1):
                for copy in third_copies(group, field):
                    copy.wait_recv()
            for plane in range(planes):
                a = orbital(band, plane)
                real, imag = potential(group, 2 * j, plane), potential(group, 2 * j + 1, plane)
                part = times(a, real, imag)
                for comp in range(comps):
                    out_ref[j, comp, plane] += part[comp]
            if last:
                out_copy(j).start()
        return carry

    if groups > 1:
        lax.fori_loop(1, groups - 1, finish, 0)
        finish(groups - 1, 0, last=True)
    else:
        for j in range(count):
            out_copy(j).start()

    for step in range(1, n_band):
        for chunk in range(chunks):
            band_copy(step, chunk).wait_send()
        for copy in rim_copies(step):
            copy.wait_send()

    def drain(group, carry):
        for chunk in range(chunks):
            for copy in halo_copies(group, chunk):
                copy.wait_send()
        for copy in edge_copies(group):
            copy.wait_send()
        for field in range(fields):
            for copy in third_copies(group, field):
                copy.wait_send()
        return carry

    lax.fori_loop(0, groups, drain, 0)
    for j in range(count):
        out_copy(j).wait()


def on_device(n_space, n_band, bands, occ_level, block_owner):
    count, comps, planes, x_rows, lanes = bands.shape
    rows = x_rows // n_band
    chunks = rows // PACK
    ext = rows + RIM
    total = count * n_band
    groups = total - count + 1
    fields = 2 * count
    peers = max(n_band - 1, 1)
    assert count == 2 and comps == 4 and planes * RIM == PACK and rows % PACK == 0
    half, full, dma = jnp.bfloat16, jnp.float32, pltpu.SemaphoreType.DMA
    return pl.pallas_call(
        functools.partial(kernel, n_space, n_band),
        out_shape=jax.ShapeDtypeStruct((count, comps, planes, rows, lanes), full),
        in_specs=[pl.BlockSpec(memory_space=pltpu.HBM)] * 3,
        out_specs=pl.BlockSpec(memory_space=pl.ANY),
        scratch_shapes=[
            pltpu.SMEM((count,), jnp.int32),
            pltpu.SMEM((1,), jnp.int32),
            pltpu.VMEM((count, comps, planes, rows, lanes), full),
            dma((2,)),
            dma((count,)),
            pltpu.VMEM((n_band, 2, count, comps, planes, PACK, lanes), half),
            pltpu.VMEM((peers, count, comps, PACK, lanes), half),
            [pltpu.VMEM((total, comps, planes, PACK, lanes), half) for chunk in range(chunks)],
            pltpu.VMEM((total, comps, PACK, lanes), half),
            pltpu.VMEM((count, 8, lanes), jnp.int32),
            pltpu.VMEM((total, 8, lanes), jnp.int32),
            pltpu.VMEM((groups, fields, planes, ext, lanes), full),
            pltpu.VMEM((groups, fields, planes, rows, lanes), half),
            pltpu.VMEM((groups, fields, PACK, lanes), half),
            pltpu.VMEM((groups, fields, planes, rows, lanes), half),
            pltpu.VMEM((groups, fields, planes, rows, lanes), half),
            pltpu.VMEM((groups, fields, PACK, lanes), half),
            pltpu.VMEM((groups, fields, PACK, lanes), half),
            pltpu.VMEM((groups, fields, planes, ext, lanes), full),
            pltpu.VMEM((2, groups, fields, rows, lanes), half),
            pltpu.VMEM((groups, fields, rows, lanes), half),
            pltpu.VMEM((groups, fields, rows, lanes), half),
            dma((n_band, 2)),
            dma((chunks,)),
            dma((peers, chunks)),
            dma((peers, chunks)),
            dma((peers,)),
            dma((peers,)),
            dma((peers,)),
            dma((peers,)),
            dma((2, groups, chunks)),
            dma((2, groups, chunks)),
            dma((2, groups)),
            dma((2, groups)),
            dma((2, groups, fields)),
            dma((2, groups, fields)),
        ],
        compiler_params=pltpu.CompilerParams(
            collective_id=0, has_side_effects=True, vmem_limit_bytes=48 * 1024 * 1024
        ),
    )(bands, occ_level, block_owner)


def solution(mesh):
    return jax.shard_map(
        functools.partial(on_device, mesh.shape["space"], mesh.shape["band"]),
        mesh=mesh,
        in_specs=(P("band", None, "space", None, None), P("band"), P()),
        out_specs=P(None, None, "space", "band", None),
        check_vma=False,
    )
```

```python
import functools
import math

import jax
import jax.numpy as jnp
from jax import lax
from jax.experimental import pallas as pl
from jax.experimental.pallas import tpu as pltpu
from jax.sharding import PartitionSpec as P

MESH = pl.DeviceIdType.MESH
jacobi_diagonal = 6.5
inverse = 1.0 / jacobi_diagonal
RIM = 8
PACK = 16


def beside(field):
    rows, lanes = field.shape
    in_x = pltpu.roll(field, 1, 0) + pltpu.roll(field, rows - 1, 0)
    return in_x + pltpu.roll(field, 1, 1) + pltpu.roll(field, lanes - 1, 1)


def kernel(
    n_space, n_band, bands_ref, occ_hbm, owner_hbm, out_hbm,
    occ_ref, owner_ref, out_ref, scalar_sem, out_sem,
    raw, rim_give, every, every_rim, occ_give, occ_every,
    dens, dens_give, dens_rim, below, above, below_rim, above_rim,
    third, third_give, third_below, third_above,
    local_sem, own_sem, band_send, band_recv, rim_send, rim_recv, occ_send, occ_recv,
    halo_send, halo_recv, edge_send, edge_recv, third_send, third_recv,
):
    count, comps, planes, x_rows, lanes = bands_ref.shape
    rows = x_rows // n_band
    chunks = rows // PACK
    total = count * n_band
    groups, fields = dens.shape[0], dens.shape[1]
    me = lax.axis_index("band")
    spot = lax.axis_index("space")
    up = lax.rem(spot + 1, n_space)
    down = lax.rem(spot + n_space - 1, n_space)
    mine = pl.ds(me * count, count)

    barrier = pltpu.get_barrier_semaphore()
    for step in range(1, n_band):
        pl.semaphore_signal(
            barrier, inc=1, device_id={"band": lax.rem(me + step, n_band)}, device_id_type=MESH
        )
    for place in (up, down):
        pl.semaphore_signal(barrier, inc=1, device_id={"space": place}, device_id_type=MESH)

    def local_copies(step):
        part = lax.rem(me + step, n_band)
        after = pl.multiple_of(lax.rem(part * rows + rows, x_rows), PACK)
        before = pl.multiple_of(lax.rem(part * rows + x_rows - PACK, x_rows), PACK)
        return [
            pltpu.make_async_copy(
                bands_ref.at[:, :, :, pl.ds(begin, PACK)], raw.at[step, side], local_sem.at[step, side]
            )
            for side, begin in enumerate((after, before))
        ]

    own_copies = [
        pltpu.make_async_copy(
            bands_ref.at[:, :, :, pl.ds(pl.multiple_of(me * rows + chunk * PACK, PACK), PACK)],
            every[chunk].at[mine],
            own_sem.at[chunk],
        )
        for chunk in range(chunks)
    ]
    for step in range(n_band):
        for copy in local_copies(step):
            copy.start()
    for copy in own_copies:
        copy.start()
    scalars = [
        pltpu.make_async_copy(occ_hbm, occ_ref, scalar_sem.at[0]),
        pltpu.make_async_copy(owner_hbm, owner_ref, scalar_sem.at[1]),
    ]
    for copy in scalars:
        copy.start()
    pl.semaphore_wait(barrier, n_band + 1)

    def band_copy(step, chunk):
        part = lax.rem(me + step, n_band)
        return pltpu.make_async_remote_copy(
            src_ref=bands_ref.at[:, :, :, pl.ds(pl.multiple_of(part * rows + chunk * PACK, PACK), PACK)],
            dst_ref=every[chunk].at[mine],
            send_sem=band_send.at[step - 1, chunk], recv_sem=band_recv.at[step - 1, chunk],
            device_id={"band": part}, device_id_type=MESH,
        )

    def rim_copies(step):
        target = {"band": lax.rem(me + step, n_band)}
        return (
            pltpu.make_async_remote_copy(
                src_ref=rim_give.at[step - 1], dst_ref=every_rim.at[mine],
                send_sem=rim_send.at[step - 1], recv_sem=rim_recv.at[step - 1],
                device_id=target, device_id_type=MESH,
            ),
            pltpu.make_async_remote_copy(
                src_ref=occ_give, dst_ref=occ_every.at[mine],
                send_sem=occ_send.at[step - 1], recv_sem=occ_recv.at[step - 1],
                device_id=target, device_id_type=MESH,
            ),
        )

    late = min(2, chunks)
    early = chunks - late
    for chunk in range(early):
        for step in range(1, n_band):
            band_copy(step, chunk).start()

    from_after = lax.broadcasted_iota(jnp.int32, (RIM, lanes), 0) < RIM // 2

    def packed_rim(step, band, comp):
        pieces = []
        for plane in range(planes):
            after = raw[step, 0, band, comp, plane].astype(jnp.float32)[:RIM]
            before = raw[step, 1, band, comp, plane].astype(jnp.float32)[RIM:]
            pieces.append(jnp.where(from_after, after, before))
        return jnp.concatenate(pieces, axis=0).astype(jnp.bfloat16)

    for step in range(n_band):
        for copy in local_copies(step):
            copy.wait()
    for copy in scalars:
        copy.wait()
    for band in range(count):
        occ_give[band] = jnp.full(occ_give.shape[1:], occ_ref[band], jnp.int32)
        occ_every[me * count + band] = jnp.full(occ_give.shape[1:], occ_ref[band], jnp.int32)
    for step in range(1, n_band):
        for band in range(count):
            for comp in range(comps):
                rim_give[step - 1, band, comp] = packed_rim(step, band, comp)
        for copy in rim_copies(step):
            copy.start()
    for chunk in range(early, chunks):
        for step in range(1, n_band):
            band_copy(step, chunk).start()
    for band in range(count):
        for comp in range(comps):
            every_rim[me * count + band, comp] = packed_rim(0, band, comp)
    for copy in own_copies:
        copy.wait()

    first = owner_ref[0]
    start = lax.div(first, count) * count
    offset = lax.rem(first, count)
    block = [start + lax.rem(offset + j, count) for j in range(count)]

    def halo_copies(group, chunk):
        return [
            pltpu.make_async_remote_copy(
                src_ref=dens_give.at[group, :, :, pl.ds(chunk * PACK, PACK)],
                dst_ref=landing.at[group, :, :, pl.ds(chunk * PACK, PACK)],
                send_sem=halo_send.at[way, group, chunk], recv_sem=halo_recv.at[way, group, chunk],
                device_id={"space": place}, device_id_type=MESH,
            )
            for way, (place, landing) in enumerate(((up, below), (down, above)))
        ]

    def edge_copies(group):
        return [
            pltpu.make_async_remote_copy(
                src_ref=dens_rim.at[group], dst_ref=landing.at[group],
                send_sem=edge_send.at[way, group], recv_sem=edge_recv.at[way, group],
                device_id={"space": place}, device_id_type=MESH,
            )
            for way, (place, landing) in enumerate(((up, below_rim), (down, above_rim)))
        ]

    def third_copies(group, field):
        return [
            pltpu.make_async_remote_copy(
                src_ref=third_give.at[1 - way, group, field], dst_ref=landing.at[group, field],
                send_sem=third_send.at[way, group, field], recv_sem=third_recv.at[way, group, field],
                device_id={"space": place}, device_id_type=MESH,
            )
            for way, (place, landing) in enumerate(((up, third_below), (down, third_above)))
        ]

    def real_part(a, b):
        return a[0] * b[0] + a[1] * b[1] + a[2] * b[2] + a[3] * b[3]

    def imag_part(a, b):
        return a[0] * b[1] - a[1] * b[0] + a[2] * b[3] - a[3] * b[2]

    def other(group):
        return lax.rem(start + count - 1 + group, total)

    def block_fields(load, keep):
        a, b = load(block[0]), load(block[1])
        keep(0, 0, real_part(a, a))
        keep(0, 1, real_part(b, b))
        keep(0, 2, real_part(a, b))
        keep(0, 3, imag_part(a, b))

    def other_fields(group, load, keep):
        c = load(other(group))
        for j in range(count):
            right = load(block[j])
            keep(group, 2 * j, real_part(c, right))
            keep(group, 2 * j + 1, imag_part(c, right))

    def chunk_io(chunk):
        span = slice(chunk * PACK, chunk * PACK + PACK)

        def load(band):
            return [
                every[chunk][band, comp].astype(jnp.float32).reshape(planes * PACK, lanes)
                for comp in range(comps)
            ]

        def keep(group, field, value):
            for plane in range(planes):
                piece = value[plane * PACK : plane * PACK + PACK]
                dens[group, field, plane, span] = piece
                dens_give[group, field, plane, span] = piece.astype(jnp.bfloat16)

        return load, keep, lambda group: halo_copies(group, chunk)

    def load_rim(band):
        return [every_rim[band, comp].astype(jnp.float32) for comp in range(comps)]

    def keep_rim(group, field, value):
        dens_rim[group, field] = value.astype(jnp.bfloat16)
        for plane in range(planes):
            dens[group, field, plane, rows : rows + RIM] = value[plane * RIM : plane * RIM + RIM]

    def stage(pieces):
        for load, keep, copies in pieces:
            block_fields(load, keep)
            for copy in copies(0):
                copy.start()

        def densities(group, carry):
            for load, keep, copies in pieces:
                other_fields(group, load, keep)
                for copy in copies(group):
                    copy.start()
            return carry

        lax.fori_loop(1, groups, densities, 0)

    for chunk in range(early):
        for step in range(1, n_band):
            band_copy(step, chunk).wait_recv()
        stage([chunk_io(chunk)])
    for step in range(1, n_band):
        for copy in rim_copies(step):
            copy.wait_recv()
    stage([(load_rim, keep_rim, edge_copies)])
    for chunk in range(early, chunks):
        for step in range(1, n_band):
            band_copy(step, chunk).wait_recv()
    stage([chunk_io(chunk) for chunk in range(early, chunks)])

    def sweeps(group, carry):
        for chunk in range(chunks):
            for copy in halo_copies(group, chunk):
                copy.wait_recv()
        for copy in edge_copies(group):
            copy.wait_recv()

        def one(field, inner):
            def landed(main, rim):
                edge = rim[group, field].astype(jnp.float32)
                return [
                    jnp.concatenate(
                        [main[group, field, k].astype(jnp.float32), edge[k * RIM : k * RIM + RIM]], axis=0
                    )
                    for k in range(planes)
                ]

            d = landed(below, below_rim)
            d += [dens[group, field, k] for k in range(planes)]
            d += landed(above, above_rim)
            second = [
                d[k] + inverse * (d[k - 1] + d[k + 1] + beside(d[k]))
                for k in range(1, planes + 3)
            ]
            for k in range(planes):
                value = d[k + 2] + inverse * (second[k] + second[k + 2] + beside(second[k + 1]))
                third[group, field, k] = value
                if k == 0:
                    third_give[0, group, field] = value[:rows].astype(jnp.bfloat16)
                if k == planes - 1:
                    third_give[1, group, field] = value[:rows].astype(jnp.bfloat16)
            for copy in third_copies(group, field):
                copy.start()
            return inner

        lax.fori_loop(0, fields, one, 0)
        return carry

    lax.fori_loop(0, groups, sweeps, 0)

    def potential(group, field, plane):
        here = third[group, field, plane]
        if plane == 0:
            low = third_below[group, field].astype(jnp.float32)
        else:
            low = third[group, field, plane - 1, 0:rows]
        if plane == planes - 1:
            high = third_above[group, field].astype(jnp.float32)
        else:
            high = third[group, field, plane + 1, 0:rows]
        return inverse * (dens[group, field, plane, 0:rows] + inverse * (low + high + beside(here)[:rows]))


    def orbital(band, plane):
        weight = occ_every[band, 0:1].astype(jnp.float32) * 0.25
        return [
            jnp.concatenate([part[band, comp, plane].astype(jnp.float32) for part in every], axis=0) * weight
            for comp in range(comps)
        ]

    def times(a, real, imag):
        parts = []
        for s in range(2):
            if imag is None:
                parts += [a[2 * s] * real, a[2 * s + 1] * real]
            else:
                parts += [a[2 * s] * real - a[2 * s + 1] * imag, a[2 * s] * imag + a[2 * s + 1] * real]
        return parts

    for field in range(fields):
        for copy in third_copies(0, field):
            copy.wait_recv()
    for plane in range(planes):
        a, b = orbital(block[0], plane), orbital(block[1], plane)
        real, imag = potential(0, 2, plane), potential(0, 3, plane)
        for j, (same, cross, sign) in enumerate(((a, b, -1.0), (b, a, 1.0))):
            one = times(same, potential(0, j, plane), None)
            two = times(cross, real, sign * imag)
            for comp in range(comps):
                out_ref[j, comp, plane] = one[comp] + two[comp]

    def out_copy(j):
        return pltpu.make_async_copy(out_ref.at[j], out_hbm.at[j], out_sem.at[j])

    def finish(group, carry, last=False):
        band = other(group)
        for j in range(count):
            for field in (2 * j, 2 * j + 1):
                for copy in third_copies(group, field):
                    copy.wait_recv()
            for plane in range(planes):
                a = orbital(band, plane)
                real, imag = potential(group, 2 * j, plane), potential(group, 2 * j + 1, plane)
                part = times(a, real, imag)
                for comp in range(comps):
                    out_ref[j, comp, plane] += part[comp]
            if last:
                out_copy(j).start()
        return carry

    if groups > 1:
        lax.fori_loop(1, groups - 1, finish, 0)
        finish(groups - 1, 0, last=True)
    else:
        for j in range(count):
            out_copy(j).start()

    for step in range(1, n_band):
        for chunk in range(chunks):
            band_copy(step, chunk).wait_send()
        for copy in rim_copies(step):
            copy.wait_send()

    def drain(group, carry):
        for chunk in range(chunks):
            for copy in halo_copies(group, chunk):
                copy.wait_send()
        for copy in edge_copies(group):
            copy.wait_send()
        for field in range(fields):
            for copy in third_copies(group, field):
                copy.wait_send()
        return carry

    lax.fori_loop(0, groups, drain, 0)
    for j in range(count):
        out_copy(j).wait()


def on_device(n_space, n_band, bands, occ_level, block_owner):
    count, comps, planes, x_rows, lanes = bands.shape
    rows = x_rows // n_band
    chunks = rows // PACK
    ext = rows + RIM
    total = count * n_band
    groups = total - count + 1
    fields = 2 * count
    peers = max(n_band - 1, 1)
    assert count == 2 and comps == 4 and planes * RIM == PACK and rows % PACK == 0
    half, full, dma = jnp.bfloat16, jnp.float32, pltpu.SemaphoreType.DMA
    sums = pl.pallas_call(
        functools.partial(kernel, n_space, n_band),
        out_shape=jax.ShapeDtypeStruct((count, comps, planes, rows, lanes), full),
        in_specs=[pl.BlockSpec(memory_space=pltpu.HBM)] * 3,
        out_specs=pl.BlockSpec(memory_space=pl.ANY),
        scratch_shapes=[
            pltpu.SMEM((count,), jnp.int32),
            pltpu.SMEM((1,), jnp.int32),
            pltpu.VMEM((count, comps, planes, rows, lanes), full),
            dma((2,)),
            dma((count,)),
            pltpu.VMEM((n_band, 2, count, comps, planes, PACK, lanes), half),
            pltpu.VMEM((peers, count, comps, PACK, lanes), half),
            [pltpu.VMEM((total, comps, planes, PACK, lanes), half) for chunk in range(chunks)],
            pltpu.VMEM((total, comps, PACK, lanes), half),
            pltpu.VMEM((count, 8, lanes), jnp.int32),
            pltpu.VMEM((total, 8, lanes), jnp.int32),
            pltpu.VMEM((groups, fields, planes, ext, lanes), full),
            pltpu.VMEM((groups, fields, planes, rows, lanes), half),
            pltpu.VMEM((groups, fields, PACK, lanes), half),
            pltpu.VMEM((groups, fields, planes, rows, lanes), half),
            pltpu.VMEM((groups, fields, planes, rows, lanes), half),
            pltpu.VMEM((groups, fields, PACK, lanes), half),
            pltpu.VMEM((groups, fields, PACK, lanes), half),
            pltpu.VMEM((groups, fields, planes, ext, lanes), full),
            pltpu.VMEM((2, groups, fields, rows, lanes), half),
            pltpu.VMEM((groups, fields, rows, lanes), half),
            pltpu.VMEM((groups, fields, rows, lanes), half),
            dma((n_band, 2)),
            dma((chunks,)),
            dma((peers, chunks)),
            dma((peers, chunks)),
            dma((peers,)),
            dma((peers,)),
            dma((peers,)),
            dma((peers,)),
            dma((2, groups, chunks)),
            dma((2, groups, chunks)),
            dma((2, groups)),
            dma((2, groups)),
            dma((2, groups, fields)),
            dma((2, groups, fields)),
        ],
        compiler_params=pltpu.CompilerParams(
            collective_id=0, has_side_effects=True, vmem_limit_bytes=65280 * 1024
        ),
    )(bands, occ_level, block_owner)
    return sums * (-1.0 / math.sqrt(total))


def solution(mesh):
    return jax.shard_map(
        functools.partial(on_device, mesh.shape["space"], mesh.shape["band"]),
        mesh=mesh,
        in_specs=(P("band", None, "space", None, None), P("band"), P()),
        out_specs=P(None, None, "space", "band", None),
        check_vma=False,
    )
```

```python
import functools
import math

import jax
import jax.numpy as jnp
from jax import lax
from jax.experimental import pallas as pl
from jax.experimental.pallas import tpu as pltpu
from jax.sharding import PartitionSpec as P

MESH = pl.DeviceIdType.MESH
jacobi_diagonal = 6.5
inverse = 1.0 / jacobi_diagonal
RIM = 8
PACK = 16


def beside(field):
    rows, lanes = field.shape
    in_x = pltpu.roll(field, 1, 0) + pltpu.roll(field, rows - 1, 0)
    return in_x + pltpu.roll(field, 1, 1) + pltpu.roll(field, lanes - 1, 1)


def pieces_of(chunks, planes):
    split = [(0, plane, 1) for plane in range(planes)] if chunks > 2 else []
    return split + [(chunk, 0, planes) for chunk in range(1 if split else 0, chunks)]


def kernel(
    n_space, n_band, bands_ref, occ_hbm, owner_hbm, out_hbm,
    occ_ref, owner_ref, out_ref, scalar_sem, out_sem,
    raw, rim_give, every, every_rim, occ_give, occ_every,
    dens, dens_give, dens_rim, below, above, below_rim, above_rim,
    third, third_give, third_below, third_above,
    local_sem, own_sem, band_send, band_recv, rim_send, rim_recv, occ_send, occ_recv,
    halo_send, halo_recv, edge_send, edge_recv, third_send, third_recv,
):
    count, comps, planes, x_rows, lanes = bands_ref.shape
    rows = x_rows // n_band
    pieces = pieces_of(rows // PACK, planes)
    total = count * n_band
    groups, fields = dens.shape[0], dens.shape[1]
    me = lax.axis_index("band")
    spot = lax.axis_index("space")
    up = lax.rem(spot + 1, n_space)
    down = lax.rem(spot + n_space - 1, n_space)
    mine = pl.ds(me * count, count)

    barrier = pltpu.get_barrier_semaphore()
    for step in range(1, n_band):
        pl.semaphore_signal(
            barrier, inc=1, device_id={"band": lax.rem(me + step, n_band)}, device_id_type=MESH
        )
    for place in (up, down):
        pl.semaphore_signal(barrier, inc=1, device_id={"space": place}, device_id_type=MESH)

    def local_copies(step):
        part = lax.rem(me + step, n_band)
        after = pl.multiple_of(lax.rem(part * rows + rows, x_rows), PACK)
        before = pl.multiple_of(lax.rem(part * rows + x_rows - PACK, x_rows), PACK)
        return [
            pltpu.make_async_copy(
                bands_ref.at[:, :, :, pl.ds(begin, PACK)], raw.at[step, side], local_sem.at[step, side]
            )
            for side, begin in enumerate((after, before))
        ]

    own_copies = [
        pltpu.make_async_copy(
            bands_ref.at[
                :, :, pl.ds(low, deep), pl.ds(pl.multiple_of(me * rows + chunk * PACK, PACK), PACK)
            ],
            every[piece].at[mine],
            own_sem.at[piece],
        )
        for piece, (chunk, low, deep) in enumerate(pieces)
    ]
    for step in range(n_band):
        for copy in local_copies(step):
            copy.start()
    for copy in own_copies:
        copy.start()
    scalars = [
        pltpu.make_async_copy(occ_hbm, occ_ref, scalar_sem.at[0]),
        pltpu.make_async_copy(owner_hbm, owner_ref, scalar_sem.at[1]),
    ]
    for copy in scalars:
        copy.start()
    pl.semaphore_wait(barrier, n_band + 1)

    def band_copy(step, piece):
        chunk, low, deep = pieces[piece]
        part = lax.rem(me + step, n_band)
        return pltpu.make_async_remote_copy(
            src_ref=bands_ref.at[
                :, :, pl.ds(low, deep), pl.ds(pl.multiple_of(part * rows + chunk * PACK, PACK), PACK)
            ],
            dst_ref=every[piece].at[mine],
            send_sem=band_send.at[step - 1, piece], recv_sem=band_recv.at[step - 1, piece],
            device_id={"band": part}, device_id_type=MESH,
        )

    def rim_copies(step):
        target = {"band": lax.rem(me + step, n_band)}
        return (
            pltpu.make_async_remote_copy(
                src_ref=rim_give.at[step - 1], dst_ref=every_rim.at[mine],
                send_sem=rim_send.at[step - 1], recv_sem=rim_recv.at[step - 1],
                device_id=target, device_id_type=MESH,
            ),
            pltpu.make_async_remote_copy(
                src_ref=occ_give, dst_ref=occ_every.at[mine],
                send_sem=occ_send.at[step - 1], recv_sem=occ_recv.at[step - 1],
                device_id=target, device_id_type=MESH,
            ),
        )

    late = min(2, len(pieces))
    early = len(pieces) - late
    for piece in range(early):
        for step in range(1, n_band):
            band_copy(step, piece).start()

    from_after = lax.broadcasted_iota(jnp.int32, (RIM, lanes), 0) < RIM // 2

    def packed_rim(step, band, comp):
        pieces = []
        for plane in range(planes):
            after = raw[step, 0, band, comp, plane].astype(jnp.float32)[:RIM]
            before = raw[step, 1, band, comp, plane].astype(jnp.float32)[RIM:]
            pieces.append(jnp.where(from_after, after, before))
        return jnp.concatenate(pieces, axis=0).astype(jnp.bfloat16)

    for step in range(n_band):
        for copy in local_copies(step):
            copy.wait()
    for copy in scalars:
        copy.wait()
    for band in range(count):
        occ_give[band] = jnp.full(occ_give.shape[1:], occ_ref[band], jnp.int32)
        occ_every[me * count + band] = jnp.full(occ_give.shape[1:], occ_ref[band], jnp.int32)
    for step in range(1, n_band):
        for band in range(count):
            for comp in range(comps):
                rim_give[step - 1, band, comp] = packed_rim(step, band, comp)
        for copy in rim_copies(step):
            copy.start()
    for piece in range(early, len(pieces)):
        for step in range(1, n_band):
            band_copy(step, piece).start()
    for band in range(count):
        for comp in range(comps):
            every_rim[me * count + band, comp] = packed_rim(0, band, comp)
    for copy in own_copies:
        copy.wait()

    first = owner_ref[0]
    start = lax.div(first, count) * count
    offset = lax.rem(first, count)
    block = [start + lax.rem(offset + j, count) for j in range(count)]

    def halo_copies(group, piece):
        chunk, low, deep = pieces[piece]
        return [
            pltpu.make_async_remote_copy(
                src_ref=dens_give.at[group, :, pl.ds(low, deep), pl.ds(chunk * PACK, PACK)],
                dst_ref=landing.at[group, :, pl.ds(low, deep), pl.ds(chunk * PACK, PACK)],
                send_sem=halo_send.at[way, group, piece], recv_sem=halo_recv.at[way, group, piece],
                device_id={"space": place}, device_id_type=MESH,
            )
            for way, (place, landing) in enumerate(((up, below), (down, above)))
        ]

    def edge_copies(group):
        return [
            pltpu.make_async_remote_copy(
                src_ref=dens_rim.at[group], dst_ref=landing.at[group],
                send_sem=edge_send.at[way, group], recv_sem=edge_recv.at[way, group],
                device_id={"space": place}, device_id_type=MESH,
            )
            for way, (place, landing) in enumerate(((up, below_rim), (down, above_rim)))
        ]

    def third_copies(group, field):
        return [
            pltpu.make_async_remote_copy(
                src_ref=third_give.at[1 - way, group, field], dst_ref=landing.at[group, field],
                send_sem=third_send.at[way, group, field], recv_sem=third_recv.at[way, group, field],
                device_id={"space": place}, device_id_type=MESH,
            )
            for way, (place, landing) in enumerate(((up, third_below), (down, third_above)))
        ]

    def real_part(a, b):
        return a[0] * b[0] + a[1] * b[1] + a[2] * b[2] + a[3] * b[3]

    def imag_part(a, b):
        return a[0] * b[1] - a[1] * b[0] + a[2] * b[3] - a[3] * b[2]

    def other(group):
        return lax.rem(start + count - 1 + group, total)

    def block_fields(load, keep):
        a, b = load(block[0]), load(block[1])
        keep(0, 0, real_part(a, a))
        keep(0, 1, real_part(b, b))
        keep(0, 2, real_part(a, b))
        keep(0, 3, imag_part(a, b))

    def other_fields(group, load, keep):
        c = load(other(group))
        for j in range(count):
            right = load(block[j])
            keep(group, 2 * j, real_part(c, right))
            keep(group, 2 * j + 1, imag_part(c, right))

    def chunk_io(piece):
        chunk, low, deep = pieces[piece]
        span = slice(chunk * PACK, chunk * PACK + PACK)

        def load(band):
            return [
                every[piece][band, comp].astype(jnp.float32).reshape(deep * PACK, lanes)
                for comp in range(comps)
            ]

        def keep(group, field, value):
            for k in range(deep):
                part = value[k * PACK : k * PACK + PACK]
                dens[group, field, low + k, span] = part
                dens_give[group, field, low + k, span] = part.astype(jnp.bfloat16)

        return load, keep, lambda group: halo_copies(group, piece)

    def load_rim(band):
        return [every_rim[band, comp].astype(jnp.float32) for comp in range(comps)]

    def keep_rim(group, field, value):
        dens_rim[group, field] = value.astype(jnp.bfloat16)
        for plane in range(planes):
            dens[group, field, plane, rows : rows + RIM] = value[plane * RIM : plane * RIM + RIM]

    def stage(pieces):
        for load, keep, copies in pieces:
            block_fields(load, keep)
            for copy in copies(0):
                copy.start()

        def densities(group, carry):
            for load, keep, copies in pieces:
                other_fields(group, load, keep)
                for copy in copies(group):
                    copy.start()
            return carry

        lax.fori_loop(1, groups, densities, 0)

    for piece in range(early):
        for step in range(1, n_band):
            band_copy(step, piece).wait_recv()
        stage([chunk_io(piece)])
    for step in range(1, n_band):
        for copy in rim_copies(step):
            copy.wait_recv()
    stage([(load_rim, keep_rim, edge_copies)])
    for piece in range(early, len(pieces)):
        for step in range(1, n_band):
            band_copy(step, piece).wait_recv()
    stage([chunk_io(piece) for piece in range(early, len(pieces))])

    def sweeps(group, carry):
        for piece in range(len(pieces)):
            for copy in halo_copies(group, piece):
                copy.wait_recv()
        for copy in edge_copies(group):
            copy.wait_recv()

        def one(field, inner):
            def landed(main, rim):
                edge = rim[group, field].astype(jnp.float32)
                return [
                    jnp.concatenate(
                        [main[group, field, k].astype(jnp.float32), edge[k * RIM : k * RIM + RIM]], axis=0
                    )
                    for k in range(planes)
                ]

            d = landed(below, below_rim)
            d += [dens[group, field, k] for k in range(planes)]
            d += landed(above, above_rim)
            second = [
                d[k] + inverse * (d[k - 1] + d[k + 1] + beside(d[k]))
                for k in range(1, planes + 3)
            ]
            for k in range(planes):
                value = d[k + 2] + inverse * (second[k] + second[k + 2] + beside(second[k + 1]))
                third[group, field, k] = value
                if k == 0:
                    third_give[0, group, field] = value[:rows].astype(jnp.bfloat16)
                if k == planes - 1:
                    third_give[1, group, field] = value[:rows].astype(jnp.bfloat16)
            for copy in third_copies(group, field):
                copy.start()
            return inner

        lax.fori_loop(0, fields, one, 0)
        return carry

    lax.fori_loop(0, groups, sweeps, 0)

    def potential(group, field, plane):
        here = third[group, field, plane]
        if plane == 0:
            low = third_below[group, field].astype(jnp.float32)
        else:
            low = third[group, field, plane - 1, 0:rows]
        if plane == planes - 1:
            high = third_above[group, field].astype(jnp.float32)
        else:
            high = third[group, field, plane + 1, 0:rows]
        return dens[group, field, plane, 0:rows] + inverse * (low + high + beside(here)[:rows])

    scale = -inverse * 0.25 / math.sqrt(total)

    def orbital(band, plane):
        weight = occ_every[band, 0:1].astype(jnp.float32) * scale
        return [
            jnp.concatenate(
                [
                    every[piece][band, comp, plane - low].astype(jnp.float32)
                    for piece, (chunk, low, deep) in enumerate(pieces)
                    if low <= plane < low + deep
                ],
                axis=0,
            )
            * weight
            for comp in range(comps)
        ]

    def times(a, real, imag):
        parts = []
        for s in range(2):
            if imag is None:
                parts += [a[2 * s] * real, a[2 * s + 1] * real]
            else:
                parts += [a[2 * s] * real - a[2 * s + 1] * imag, a[2 * s] * imag + a[2 * s + 1] * real]
        return parts

    for field in range(fields):
        for copy in third_copies(0, field):
            copy.wait_recv()
    for plane in range(planes):
        a, b = orbital(block[0], plane), orbital(block[1], plane)
        real, imag = potential(0, 2, plane), potential(0, 3, plane)
        for j, (same, cross, sign) in enumerate(((a, b, -1.0), (b, a, 1.0))):
            one = times(same, potential(0, j, plane), None)
            two = times(cross, real, sign * imag)
            for comp in range(comps):
                out_ref[j, comp, plane] = one[comp] + two[comp]

    def out_copy(j):
        return pltpu.make_async_copy(out_ref.at[j], out_hbm.at[j], out_sem.at[j])

    def finish(group, carry, last=False):
        band = other(group)
        for j in range(count):
            for field in (2 * j, 2 * j + 1):
                for copy in third_copies(group, field):
                    copy.wait_recv()
            for plane in range(planes):
                a = orbital(band, plane)
                real, imag = potential(group, 2 * j, plane), potential(group, 2 * j + 1, plane)
                part = times(a, real, imag)
                for comp in range(comps):
                    out_ref[j, comp, plane] += part[comp]
            if last:
                out_copy(j).start()
        return carry

    if groups > 1:
        lax.fori_loop(1, groups - 1, finish, 0)
        finish(groups - 1, 0, last=True)
    else:
        for j in range(count):
            out_copy(j).start()

    for step in range(1, n_band):
        for piece in range(len(pieces)):
            band_copy(step, piece).wait_send()
        for copy in rim_copies(step):
            copy.wait_send()

    def drain(group, carry):
        for piece in range(len(pieces)):
            for copy in halo_copies(group, piece):
                copy.wait_send()
        for copy in edge_copies(group):
            copy.wait_send()
        for field in range(fields):
            for copy in third_copies(group, field):
                copy.wait_send()
        return carry

    lax.fori_loop(0, groups, drain, 0)
    for j in range(count):
        out_copy(j).wait()


def on_device(n_space, n_band, bands, occ_level, block_owner):
    count, comps, planes, x_rows, lanes = bands.shape
    rows = x_rows // n_band
    pieces = pieces_of(rows // PACK, planes)
    ext = rows + RIM
    total = count * n_band
    groups = total - count + 1
    fields = 2 * count
    peers = max(n_band - 1, 1)
    assert count == 2 and comps == 4 and planes * RIM == PACK and rows % PACK == 0
    half, full, dma = jnp.bfloat16, jnp.float32, pltpu.SemaphoreType.DMA
    return pl.pallas_call(
        functools.partial(kernel, n_space, n_band),
        out_shape=jax.ShapeDtypeStruct((count, comps, planes, rows, lanes), full),
        in_specs=[pl.BlockSpec(memory_space=pltpu.HBM)] * 3,
        out_specs=pl.BlockSpec(memory_space=pl.ANY),
        scratch_shapes=[
            pltpu.SMEM((count,), jnp.int32),
            pltpu.SMEM((1,), jnp.int32),
            pltpu.VMEM((count, comps, planes, rows, lanes), full),
            dma((2,)),
            dma((count,)),
            pltpu.VMEM((n_band, 2, count, comps, planes, PACK, lanes), half),
            pltpu.VMEM((peers, count, comps, PACK, lanes), half),
            [pltpu.VMEM((total, comps, deep, PACK, lanes), half) for chunk, low, deep in pieces],
            pltpu.VMEM((total, comps, PACK, lanes), half),
            pltpu.VMEM((count, 8, lanes), jnp.int32),
            pltpu.VMEM((total, 8, lanes), jnp.int32),
            pltpu.VMEM((groups, fields, planes, ext, lanes), full),
            pltpu.VMEM((groups, fields, planes, rows, lanes), half),
            pltpu.VMEM((groups, fields, PACK, lanes), half),
            pltpu.VMEM((groups, fields, planes, rows, lanes), half),
            pltpu.VMEM((groups, fields, planes, rows, lanes), half),
            pltpu.VMEM((groups, fields, PACK, lanes), half),
            pltpu.VMEM((groups, fields, PACK, lanes), half),
            pltpu.VMEM((groups, fields, planes, ext, lanes), full),
            pltpu.VMEM((2, groups, fields, rows, lanes), half),
            pltpu.VMEM((groups, fields, rows, lanes), half),
            pltpu.VMEM((groups, fields, rows, lanes), half),
            dma((n_band, 2)),
            dma((len(pieces),)),
            dma((peers, len(pieces))),
            dma((peers, len(pieces))),
            dma((peers,)),
            dma((peers,)),
            dma((peers,)),
            dma((peers,)),
            dma((2, groups, len(pieces))),
            dma((2, groups, len(pieces))),
            dma((2, groups)),
            dma((2, groups)),
            dma((2, groups, fields)),
            dma((2, groups, fields)),
        ],
        compiler_params=pltpu.CompilerParams(
            collective_id=0, has_side_effects=True, vmem_limit_bytes=48 * 1024 * 1024
        ),
    )(bands, occ_level, block_owner)


def solution(mesh):
    return jax.shard_map(
        functools.partial(on_device, mesh.shape["space"], mesh.shape["band"]),
        mesh=mesh,
        in_specs=(P("band", None, "space", None, None), P("band"), P()),
        out_specs=P(None, None, "space", "band", None),
        check_vma=False,
    )
```

```python
import functools
import math

import jax
import jax.numpy as jnp
from jax import lax
from jax.experimental import pallas as pl
from jax.experimental.pallas import tpu as pltpu
from jax.sharding import PartitionSpec as P

MESH = pl.DeviceIdType.MESH
jacobi_diagonal = 6.5
inverse = 1.0 / jacobi_diagonal
RIM = 8
PACK = 16


def beside(field):
    rows, lanes = field.shape
    in_x = pltpu.roll(field, 1, 0) + pltpu.roll(field, rows - 1, 0)
    return in_x + pltpu.roll(field, 1, 1) + pltpu.roll(field, lanes - 1, 1)


def kernel(
    n_space, n_band, bands_ref, occ_hbm, owner_hbm, out_ref,
    occ_ref, owner_ref, scalar_sem,
    raw, rim_give, every, every_rim, occ_give, occ_every,
    dens, dens_give, dens_rim, below, above, below_rim, above_rim,
    third, third_give, third_below, third_above,
    local_sem, own_sem, band_send, band_recv, rim_send, rim_recv, occ_send, occ_recv,
    halo_send, halo_recv, edge_send, edge_recv, third_send, third_recv,
):
    count, comps, planes, x_rows, lanes = bands_ref.shape
    rows = x_rows // n_band
    chunks = rows // PACK
    total = count * n_band
    groups, fields = dens.shape[0], dens.shape[1]
    me = lax.axis_index("band")
    spot = lax.axis_index("space")
    up = lax.rem(spot + 1, n_space)
    down = lax.rem(spot + n_space - 1, n_space)
    mine = pl.ds(me * count, count)

    barrier = pltpu.get_barrier_semaphore()
    for step in range(1, n_band):
        pl.semaphore_signal(
            barrier, inc=1, device_id={"band": lax.rem(me + step, n_band)}, device_id_type=MESH
        )
    for place in (up, down):
        pl.semaphore_signal(barrier, inc=1, device_id={"space": place}, device_id_type=MESH)

    def local_copies(step):
        part = lax.rem(me + step, n_band)
        after = pl.multiple_of(lax.rem(part * rows + rows, x_rows), PACK)
        before = pl.multiple_of(lax.rem(part * rows + x_rows - PACK, x_rows), PACK)
        return [
            pltpu.make_async_copy(
                bands_ref.at[:, :, :, pl.ds(begin, PACK)], raw.at[step, side], local_sem.at[step, side]
            )
            for side, begin in enumerate((after, before))
        ]

    own_copies = [
        pltpu.make_async_copy(
            bands_ref.at[:, :, :, pl.ds(pl.multiple_of(me * rows + chunk * PACK, PACK), PACK)],
            every[chunk].at[mine],
            own_sem.at[chunk],
        )
        for chunk in range(chunks)
    ]
    for step in range(n_band):
        for copy in local_copies(step):
            copy.start()
    for copy in own_copies:
        copy.start()
    scalars = [
        pltpu.make_async_copy(occ_hbm, occ_ref, scalar_sem.at[0]),
        pltpu.make_async_copy(owner_hbm, owner_ref, scalar_sem.at[1]),
    ]
    for copy in scalars:
        copy.start()
    pl.semaphore_wait(barrier, n_band + 1)

    def band_copy(step, chunk):
        part = lax.rem(me + step, n_band)
        return pltpu.make_async_remote_copy(
            src_ref=bands_ref.at[:, :, :, pl.ds(pl.multiple_of(part * rows + chunk * PACK, PACK), PACK)],
            dst_ref=every[chunk].at[mine],
            send_sem=band_send.at[step - 1, chunk], recv_sem=band_recv.at[step - 1, chunk],
            device_id={"band": part}, device_id_type=MESH,
        )

    def rim_copies(step):
        target = {"band": lax.rem(me + step, n_band)}
        return (
            pltpu.make_async_remote_copy(
                src_ref=rim_give.at[step - 1], dst_ref=every_rim.at[mine],
                send_sem=rim_send.at[step - 1], recv_sem=rim_recv.at[step - 1],
                device_id=target, device_id_type=MESH,
            ),
            pltpu.make_async_remote_copy(
                src_ref=occ_give, dst_ref=occ_every.at[mine],
                send_sem=occ_send.at[step - 1], recv_sem=occ_recv.at[step - 1],
                device_id=target, device_id_type=MESH,
            ),
        )

    late = min(2, chunks)
    early = chunks - late
    for chunk in range(early):
        for step in range(1, n_band):
            band_copy(step, chunk).start()

    from_after = lax.broadcasted_iota(jnp.int32, (RIM, lanes), 0) < RIM // 2

    def packed_rim(step, band, comp):
        pieces = []
        for plane in range(planes):
            after = raw[step, 0, band, comp, plane].astype(jnp.float32)[:RIM]
            before = raw[step, 1, band, comp, plane].astype(jnp.float32)[RIM:]
            pieces.append(jnp.where(from_after, after, before))
        return jnp.concatenate(pieces, axis=0).astype(jnp.bfloat16)

    for step in range(n_band):
        for copy in local_copies(step):
            copy.wait()
    for copy in scalars:
        copy.wait()
    for band in range(count):
        occ_give[band] = jnp.full(occ_give.shape[1:], occ_ref[band], jnp.int32)
        occ_every[me * count + band] = jnp.full(occ_give.shape[1:], occ_ref[band], jnp.int32)
    for step in range(1, n_band):
        for band in range(count):
            for comp in range(comps):
                rim_give[step - 1, band, comp] = packed_rim(step, band, comp)
        for copy in rim_copies(step):
            copy.start()
    for chunk in range(early, chunks):
        for step in range(1, n_band):
            band_copy(step, chunk).start()
    for band in range(count):
        for comp in range(comps):
            every_rim[me * count + band, comp] = packed_rim(0, band, comp)
    for copy in own_copies:
        copy.wait()

    first = owner_ref[0]
    start = lax.div(first, count) * count
    offset = lax.rem(first, count)
    block = [start + lax.rem(offset + j, count) for j in range(count)]

    def halo_copies(group, chunk):
        return [
            pltpu.make_async_remote_copy(
                src_ref=dens_give.at[group, :, :, pl.ds(chunk * PACK, PACK)],
                dst_ref=landing.at[group, :, :, pl.ds(chunk * PACK, PACK)],
                send_sem=halo_send.at[way, group, chunk], recv_sem=halo_recv.at[way, group, chunk],
                device_id={"space": place}, device_id_type=MESH,
            )
            for way, (place, landing) in enumerate(((up, below), (down, above)))
        ]

    def edge_copies(group):
        return [
            pltpu.make_async_remote_copy(
                src_ref=dens_rim.at[group], dst_ref=landing.at[group],
                send_sem=edge_send.at[way, group], recv_sem=edge_recv.at[way, group],
                device_id={"space": place}, device_id_type=MESH,
            )
            for way, (place, landing) in enumerate(((up, below_rim), (down, above_rim)))
        ]

    def third_copies(group, field):
        return [
            pltpu.make_async_remote_copy(
                src_ref=third_give.at[1 - way, group, field], dst_ref=landing.at[group, field],
                send_sem=third_send.at[way, group, field], recv_sem=third_recv.at[way, group, field],
                device_id={"space": place}, device_id_type=MESH,
            )
            for way, (place, landing) in enumerate(((up, third_below), (down, third_above)))
        ]

    def real_part(a, b):
        return a[0] * b[0] + a[1] * b[1] + a[2] * b[2] + a[3] * b[3]

    def imag_part(a, b):
        return a[0] * b[1] - a[1] * b[0] + a[2] * b[3] - a[3] * b[2]

    def other(group):
        return lax.rem(start + count - 1 + group, total)

    def block_fields(load, keep):
        a, b = load(block[0]), load(block[1])
        keep(0, 0, real_part(a, a))
        keep(0, 1, real_part(b, b))
        keep(0, 2, real_part(a, b))
        keep(0, 3, imag_part(a, b))

    def other_fields(group, load, keep):
        c = load(other(group))
        for j in range(count):
            right = load(block[j])
            keep(group, 2 * j, real_part(c, right))
            keep(group, 2 * j + 1, imag_part(c, right))

    def chunk_io(chunk):
        span = slice(chunk * PACK, chunk * PACK + PACK)

        def load(band):
            return [
                every[chunk][band, comp].astype(jnp.float32).reshape(planes * PACK, lanes)
                for comp in range(comps)
            ]

        def keep(group, field, value):
            for plane in range(planes):
                piece = value[plane * PACK : plane * PACK + PACK]
                dens[group, field, plane, span] = piece
                dens_give[group, field, plane, span] = piece.astype(jnp.bfloat16)

        return load, keep, lambda group: halo_copies(group, chunk)

    def load_rim(band):
        return [every_rim[band, comp].astype(jnp.float32) for comp in range(comps)]

    def keep_rim(group, field, value):
        dens_rim[group, field] = value.astype(jnp.bfloat16)
        for plane in range(planes):
            dens[group, field, plane, rows : rows + RIM] = value[plane * RIM : plane * RIM + RIM]

    def stage(pieces):
        for load, keep, copies in pieces:
            block_fields(load, keep)
            for copy in copies(0):
                copy.start()

        def densities(group, carry):
            for load, keep, copies in pieces:
                other_fields(group, load, keep)
                for copy in copies(group):
                    copy.start()
            return carry

        lax.fori_loop(1, groups, densities, 0)

    for chunk in range(early):
        for step in range(1, n_band):
            band_copy(step, chunk).wait_recv()
        stage([chunk_io(chunk)])
    for step in range(1, n_band):
        for copy in rim_copies(step):
            copy.wait_recv()
    stage([(load_rim, keep_rim, edge_copies)])
    for chunk in range(early, chunks):
        for step in range(1, n_band):
            band_copy(step, chunk).wait_recv()
    stage([chunk_io(chunk) for chunk in range(early, chunks)])

    def sweeps(group, carry):
        for chunk in range(chunks):
            for copy in halo_copies(group, chunk):
                copy.wait_recv()
        for copy in edge_copies(group):
            copy.wait_recv()

        def one(field, inner):
            def landed(main, rim):
                edge = rim[group, field].astype(jnp.float32)
                return [
                    jnp.concatenate(
                        [main[group, field, k].astype(jnp.float32), edge[k * RIM : k * RIM + RIM]], axis=0
                    )
                    for k in range(planes)
                ]

            d = landed(below, below_rim)
            d += [dens[group, field, k] for k in range(planes)]
            d += landed(above, above_rim)
            second = [
                d[k] + inverse * (d[k - 1] + d[k + 1] + beside(d[k]))
                for k in range(1, planes + 3)
            ]
            for k in range(planes):
                value = d[k + 2] + inverse * (second[k] + second[k + 2] + beside(second[k + 1]))
                third[group, field, k] = value
                if k == 0:
                    third_give[0, group, field] = value[:rows].astype(jnp.bfloat16)
                if k == planes - 1:
                    third_give[1, group, field] = value[:rows].astype(jnp.bfloat16)
            for copy in third_copies(group, field):
                copy.start()
            return inner

        lax.fori_loop(0, fields, one, 0)
        return carry

    lax.fori_loop(0, groups, sweeps, 0)

    def potential(group, field, plane):
        here = third[group, field, plane]
        if plane == 0:
            low = third_below[group, field].astype(jnp.float32)
        else:
            low = third[group, field, plane - 1, 0:rows]
        if plane == planes - 1:
            high = third_above[group, field].astype(jnp.float32)
        else:
            high = third[group, field, plane + 1, 0:rows]
        return dens[group, field, plane, 0:rows] + inverse * (low + high + beside(here)[:rows])

    scale = -inverse * 0.25 / math.sqrt(total)

    def orbital(band, plane):
        weight = occ_every[band, 0:1].astype(jnp.float32) * scale
        return [
            jnp.concatenate([part[band, comp, plane].astype(jnp.float32) for part in every], axis=0) * weight
            for comp in range(comps)
        ]

    def times(a, real, imag):
        parts = []
        for s in range(2):
            if imag is None:
                parts += [a[2 * s] * real, a[2 * s + 1] * real]
            else:
                parts += [a[2 * s] * real - a[2 * s + 1] * imag, a[2 * s] * imag + a[2 * s + 1] * real]
        return parts

    for step in range(1, n_band):
        for chunk in range(chunks):
            band_copy(step, chunk).wait_send()
        for copy in rim_copies(step):
            copy.wait_send()

    def halo_sent(group, carry):
        for chunk in range(chunks):
            for copy in halo_copies(group, chunk):
                copy.wait_send()
        for copy in edge_copies(group):
            copy.wait_send()
        return carry

    lax.fori_loop(0, groups, halo_sent, 0)
    for field in range(fields):
        for copy in third_copies(0, field):
            copy.wait_recv()
    for plane in range(planes):
        a, b = orbital(block[0], plane), orbital(block[1], plane)
        real, imag = potential(0, 2, plane), potential(0, 3, plane)
        for j, (same, cross, sign) in enumerate(((a, b, -1.0), (b, a, 1.0))):
            one = times(same, potential(0, j, plane), None)
            two = times(cross, real, sign * imag)
            for comp in range(comps):
                out_ref[j, comp, plane] = one[comp] + two[comp]

    def finish(group, carry):
        band = other(group)
        for j in range(count):
            for field in (2 * j, 2 * j + 1):
                for copy in third_copies(group, field):
                    copy.wait_recv()
            for plane in range(planes):
                a = orbital(band, plane)
                real, imag = potential(group, 2 * j, plane), potential(group, 2 * j + 1, plane)
                part = times(a, real, imag)
                for comp in range(comps):
                    out_ref[j, comp, plane] += part[comp]
        return carry

    def third_sent(group, carry):
        for field in range(fields):
            for copy in third_copies(group, field):
                copy.wait_send()
        return carry

    if groups > 1:
        lax.fori_loop(1, groups - 1, finish, 0)
        lax.fori_loop(0, groups - 1, third_sent, 0)
        finish(groups - 1, 0)
    third_sent(groups - 1, 0)


def on_device(n_space, n_band, bands, occ_level, block_owner):
    count, comps, planes, x_rows, lanes = bands.shape
    rows = x_rows // n_band
    chunks = rows // PACK
    ext = rows + RIM
    total = count * n_band
    groups = total - count + 1
    fields = 2 * count
    peers = max(n_band - 1, 1)
    assert count == 2 and comps == 4 and planes * RIM == PACK and rows % PACK == 0
    half, full, dma = jnp.bfloat16, jnp.float32, pltpu.SemaphoreType.DMA
    return pl.pallas_call(
        functools.partial(kernel, n_space, n_band),
        out_shape=jax.ShapeDtypeStruct((count, comps, planes, rows, lanes), full),
        in_specs=[pl.BlockSpec(memory_space=pltpu.HBM)] * 3,
        out_specs=pl.BlockSpec(memory_space=pltpu.VMEM),
        scratch_shapes=[
            pltpu.SMEM((count,), jnp.int32),
            pltpu.SMEM((1,), jnp.int32),
            dma((2,)),
            pltpu.VMEM((n_band, 2, count, comps, planes, PACK, lanes), half),
            pltpu.VMEM((peers, count, comps, PACK, lanes), half),
            [pltpu.VMEM((total, comps, planes, PACK, lanes), half) for chunk in range(chunks)],
            pltpu.VMEM((total, comps, PACK, lanes), half),
            pltpu.VMEM((count, 8, lanes), jnp.int32),
            pltpu.VMEM((total, 8, lanes), jnp.int32),
            pltpu.VMEM((groups, fields, planes, ext, lanes), full),
            pltpu.VMEM((groups, fields, planes, rows, lanes), half),
            pltpu.VMEM((groups, fields, PACK, lanes), half),
            pltpu.VMEM((groups, fields, planes, rows, lanes), half),
            pltpu.VMEM((groups, fields, planes, rows, lanes), half),
            pltpu.VMEM((groups, fields, PACK, lanes), half),
            pltpu.VMEM((groups, fields, PACK, lanes), half),
            pltpu.VMEM((groups, fields, planes, ext, lanes), full),
            pltpu.VMEM((2, groups, fields, rows, lanes), half),
            pltpu.VMEM((groups, fields, rows, lanes), half),
            pltpu.VMEM((groups, fields, rows, lanes), half),
            dma((n_band, 2)),
            dma((chunks,)),
            dma((peers, chunks)),
            dma((peers, chunks)),
            dma((peers,)),
            dma((peers,)),
            dma((peers,)),
            dma((peers,)),
            dma((2, groups, chunks)),
            dma((2, groups, chunks)),
            dma((2, groups)),
            dma((2, groups)),
            dma((2, groups, fields)),
            dma((2, groups, fields)),
        ],
        compiler_params=pltpu.CompilerParams(
            collective_id=0, has_side_effects=True, vmem_limit_bytes=48 * 1024 * 1024
        ),
    )(bands, occ_level, block_owner)


def solution(mesh):
    return jax.shard_map(
        functools.partial(on_device, mesh.shape["space"], mesh.shape["band"]),
        mesh=mesh,
        in_specs=(P("band", None, "space", None, None), P("band"), P()),
        out_specs=P(None, None, "space", "band", None),
        check_vma=False,
    )
```
